128 devices in a mesh: src: 16 (over z, y), tgt: 8 (over x, core).
Axes of the slice: x: 4, y: 4, z: 4, core: 2. Of those that a mesh axis runs over, the one named last changes fastest.
Arguments:
- src_points: float32 [3, 2097152], P(None, ('src', 'tgt'))
- tgt_points: float32 [3, 2097152], P(None, ('src', 'tgt'))
- src_count: int32 [8192], P(('src', 'tgt')), may hold values from 128 to 256
- tgt_count: int32 [8192], P(('src', 'tgt')), may hold values from 128 to 256
- pair_list: int32 [2, 40960], P(None, ('src', 'tgt')), may hold values from 0 to 67, as said below
- pair_total: int32 [128], P(('src', 'tgt')), may hold values from 1 to 320, as said below
- rhs: float32 [8, 2097152], P(None, ('src', 'tgt'))
Outputs:
- coefficients: float32 [8, 2097152], P(None, ('src', 'tgt'))
- mapped: float32 [8, 2097152], P(None, ('src', 'tgt'))
The draws below stay inside these ranges and needn't reach their ends.
Inputs may be any that keep to these rules, and one draw needn't show every extreme that they name: `pair_list`: pair (a, b) in a device's numbering has a among its own 64 blocks and 0 <= b - a <= 4, where b >= 64 names block b - 64 of the next device. Every pair of blocks in which a source or target point lies within distance 4 of a source point of the other is listed exactly once, by the device that holds the lower block; listed pairs may also include blocks with no such points. Slots from pair_total on hold (0, 0). `pair_total`: some device has all 320 slots live in every draw.
All inputs are finite; a program needn't handle non-finite values.
Results may differ from the reference program's by a relative error of at most 0.0003.
Values sent between devices are 32-bit elements; how exact they have to be, the bound alone decides.
A program may use at most 64 MiB of HBM per device.

```python
import jax
import jax.numpy as jnp
from jax import lax

BP = 256
F = 8
R = 4
ITERS = 2
BLK_DEV = 64
PAIRS_DEV = 320
NB = 8192
NPTS = 2097152
N_SRC = 16
N_TGT = 8


def block_layout(key):
    devices = N_SRC * N_TGT
    keys = jax.random.split(jax.random.fold_in(key, 101), 3)
    dense = jax.random.randint(keys[0], (devices,), 0, 8) == 0
    chosen = jax.random.randint(keys[1], (), 0, devices - 1)
    ranks = jnp.arange(devices)
    dense = dense | (ranks == chosen) | (ranks == chosen + 1) | (ranks >= devices - 2)
    spread_widths = jax.random.randint(keys[2], (devices, BLK_DEV), R, 2 * R + 1)
    widths = jnp.where(dense[:, None], 1, spread_widths).reshape(-1).astype(jnp.int32)
    starts = (jnp.cumsum(widths) - widths).astype(jnp.int32)
    return (widths, starts)


def pair_layout(key):
    devices = N_SRC * N_TGT
    widths, starts = block_layout(key)
    blocks = widths.shape[0]
    lower = jnp.arange(blocks).astype(jnp.int32)[:, None]
    reach = jnp.arange(R + 1).astype(jnp.int32)[None, :]
    upper = lower + reach
    inside = upper < blocks
    upper_safe = jnp.minimum(upper, blocks - 1)
    distance_gap = starts[upper_safe] - (starts[lower] + widths[lower])
    live = (inside & (distance_gap < R)).reshape(devices, PAIRS_DEV)
    index = jnp.arange(PAIRS_DEV).astype(jnp.int32)[None, :]
    scores = jnp.where(live, 0, 1).astype(jnp.int32) * PAIRS_DEV + index
    order = jnp.argsort(scores, axis=1).astype(jnp.int32)
    live_sorted = jnp.take_along_axis(live, order, axis=1)
    local_lower = order // (R + 1) % BLK_DEV
    local_upper = local_lower + order % (R + 1)
    local_lower = jnp.where(live_sorted, local_lower, 0)
    local_upper = jnp.where(live_sorted, local_upper, 0)
    listing = jnp.stack([local_lower, local_upper], 0).reshape(2, devices * PAIRS_DEV).astype(jnp.int32)
    totals = jnp.sum(live.astype(jnp.int32), axis=1).astype(jnp.int32)
    return (listing, totals)


def place_points(key, salt):
    widths, starts = block_layout(key)
    key = jax.random.fold_in(key, salt)
    keys = jax.random.split(key, 3)
    along = jax.random.uniform(keys[0], (NB, BP), jnp.float32)
    across = jax.random.uniform(keys[1], (NB, BP), jnp.float32) * float(BP)
    height = jax.random.uniform(keys[2], (NB, BP), jnp.float32) * 2.0
    first_coord = starts[:, None].astype(jnp.float32) + along * widths[:, None].astype(jnp.float32)
    return jnp.stack([first_coord, across, height], 0).reshape(3, NPTS)


def draw_src_points(key, part):
    return place_points(key, 5)


def draw_tgt_points(key, part):
    return place_points(key, 7)


def draw_pair_list(key, part):
    return pair_layout(key)[0]


def draw_pair_total(key, part):
    return pair_layout(key)[1]


def draw_rhs(key, part):
    key = jax.random.fold_in(key, 17)
    keys = jax.random.split(key, 1)
    position = jnp.arange(NPTS).astype(jnp.float32) / NPTS
    base = jnp.clip(jax.random.normal(keys[0], (F, NPTS), jnp.float32), -4.0, 4.0)
    return base * (1.0 + 2.0 * position)[None, :]


def touch_ends(values, stream_key, smallest, largest):
    place = [jax.random.randint(jax.random.fold_in(stream_key, axis), (), 0, length) for axis, length in enumerate(values.shape)]
    widest = values.shape.index(max(values.shape))
    neighbour = place[:widest] + [(place[widest] + 1) % values.shape[widest]] + place[widest + 1:]
    return values.at[tuple(place)].set(smallest).at[tuple(neighbour)].set(largest)


def setup_inputs(seed: int = 0) -> dict:
    splits = jax.random.split(jax.random.key(seed), 8)
    src_points = draw_src_points(jax.random.fold_in(splits[7], 71), 0)
    tgt_points = draw_tgt_points(jax.random.fold_in(splits[7], 71), 0)
    src_count = touch_ends(jax.random.randint(splits[2], (NB,), BP // 2, BP + 1), jax.random.fold_in(splits[2], 1), BP // 2, BP).astype(jnp.int32)
    tgt_count = touch_ends(jax.random.randint(splits[3], (NB,), BP // 2, BP + 1), jax.random.fold_in(splits[3], 1), BP // 2, BP).astype(jnp.int32)
    pair_list = draw_pair_list(jax.random.fold_in(splits[7], 71), 0)
    pair_total = draw_pair_total(jax.random.fold_in(splits[7], 71), 0)
    rhs = draw_rhs(jax.random.fold_in(splits[7], 71), 0)
    return dict(src_points=src_points, tgt_points=tgt_points, src_count=src_count, tgt_count=tgt_count, pair_list=pair_list, pair_total=pair_total, rhs=rhs)


batch_pairs = 64

def wendland(left, right, left_mask, right_mask):
    offset = left[:, 0, :, None] - right[:, 0, None, :]
    distance = offset * offset
    for axis_number in (1, 2):
        offset = left[:, axis_number, :, None] - right[:, axis_number, None, :]
        distance = distance + offset * offset
    scaled = jnp.sqrt(distance) * (1.0 / R)
    remain = jnp.maximum(1.0 - scaled, 0.0)
    squared = remain * remain
    return squared * squared * (5.0 - 4.0 * remain) * left_mask[:, :, None] * right_mask[:, None, :]

def reference(src_points, tgt_points, src_count, tgt_count, pair_list, pair_total, rhs):
    devices = N_SRC * N_TGT
    blocks = BLK_DEV * devices
    source = src_points.reshape(3, blocks, BP).transpose(1, 0, 2)
    target = tgt_points.reshape(3, blocks, BP).transpose(1, 0, 2)
    slots = jnp.arange(BP).astype(jnp.int32)
    source_mask = (slots[None, :] < src_count[:, None]).astype(jnp.float32)
    target_mask = (slots[None, :] < tgt_count[:, None]).astype(jnp.float32)
    total = devices * PAIRS_DEV
    column = jnp.arange(total).astype(jnp.int32)
    owner = column // PAIRS_DEV
    first = pair_list[0] + owner * BLK_DEV
    second = pair_list[1] + owner * BLK_DEV
    live = (column % PAIRS_DEV < pair_total[owner]).astype(jnp.float32)
    forward = live
    backward = live * (first != second).astype(jnp.float32)
    groups = -(-total // batch_pairs)
    extra = groups * batch_pairs - total
    first = jnp.pad(first, (0, extra)).reshape(groups, batch_pairs)
    second = jnp.pad(second, (0, extra)).reshape(groups, batch_pairs)
    forward = jnp.pad(forward, (0, extra)).reshape(groups, batch_pairs)
    backward = jnp.pad(backward, (0, extra)).reshape(groups, batch_pairs)
    highest = lax.Precision.HIGHEST

    def apply_operator(values):

        def step_pairs(acc, item):
            lower, upper, weight_f, weight_b = item
            kernel = wendland(source[lower], source[upper], source_mask[lower], source_mask[upper])
            ahead = jnp.einsum('gij,fgj->fgi', kernel, values[:, upper], precision=highest) * weight_f[None, :, None]
            behind = jnp.einsum('gij,fgi->fgj', kernel, values[:, lower], precision=highest) * weight_b[None, :, None]
            acc = acc.at[:, lower].add(ahead)
            acc = acc.at[:, upper].add(behind)
            return (acc, None)
        start_acc = jnp.zeros((F, blocks, BP), jnp.float32)
        return lax.scan(step_pairs, start_acc, (first, second, forward, backward))[0]

    def apply_evaluation(values):

        def step_pairs(acc, item):
            lower, upper, weight_f, weight_b = item
            kernel_f = wendland(target[lower], source[upper], target_mask[lower], source_mask[upper])
            kernel_b = wendland(target[upper], source[lower], target_mask[upper], source_mask[lower])
            ahead = jnp.einsum('gij,fgj->fgi', kernel_f, values[:, upper], precision=highest) * weight_f[None, :, None]
            behind = jnp.einsum('gij,fgj->fgi', kernel_b, values[:, lower], precision=highest) * weight_b[None, :, None]
            acc = acc.at[:, lower].add(ahead)
            acc = acc.at[:, upper].add(behind)
            return (acc, None)
        start_acc = jnp.zeros((F, blocks, BP), jnp.float32)
        return lax.scan(step_pairs, start_acc, (first, second, forward, backward))[0]
    field = rhs.reshape(F, blocks, BP) * source_mask[None]
    solution = jnp.zeros_like(field)
    residual = field
    direction = field
    norm_now = lax.optimization_barrier(jnp.sum(residual * residual, axis=(1, 2)))
    for step in range(ITERS):
        image = apply_operator(direction)
        alpha = norm_now / lax.optimization_barrier(jnp.sum(direction * image, axis=(1, 2)))
        solution = solution + alpha[:, None, None] * direction
        residual = residual - alpha[:, None, None] * image
        norm_next = lax.optimization_barrier(jnp.sum(residual * residual, axis=(1, 2)))
        direction = residual + (norm_next / norm_now)[:, None, None] * direction
        norm_now = norm_next
    mapped = apply_evaluation(solution)
    return (solution.reshape(F, blocks * BP), mapped.reshape(F, blocks * BP))
```

```python
import functools

import jax
import jax.numpy as jnp
from jax import lax
from jax.experimental import pallas as pl
from jax.experimental.pallas import tpu as pltpu
from jax.sharding import PartitionSpec as P

R = 4
BP = 256
F = 8
GS = R * BP
HALO = 2
LANES = 128
CHUNKS = GS // LANES
BINS = 128
WIN = 192
ROW_STRIDE = GS + WIN
VAL_STRIDE = GS + 384
SEG = 256
AXES = ("src", "tgt")
f32 = jnp.float32
bf16 = jnp.bfloat16
i32 = jnp.int32


def iota(shape, dim):
    return lax.broadcasted_iota(i32, shape, dim)


def dot(a, b, dims=((1,), (0,))):
    return lax.dot_general(a, b, (dims, ((), ())), preferred_element_type=f32)


def slot_mask(cnt_ref, group):
    slot = iota((1, GS), 1)
    block = slot // BP
    limit = jnp.zeros((1, GS), i32)
    for k in range(R):
        limit = jnp.where(block == k, cnt_ref[group * R + k], limit)
    return (slot % BP) < limit


def live_total(cnt_ref, group):
    total = cnt_ref[group * R]
    for k in range(1, R):
        total = total + cnt_ref[group * R + k]
    return total


def order(y, live):
    low = jnp.min(jnp.where(live, y, jnp.inf))
    high = jnp.max(jnp.where(live, y, -jnp.inf))
    scale = BINS / jnp.maximum(high - low, 1e-30)
    scaled = jnp.minimum(jnp.maximum((y - low) * scale, 0.0), BINS - 1.0)
    bin_of = jnp.where(live, scaled.astype(i32), BINS)
    ones_col = iota((SEG, SEG + LANES), 1)
    upper = ((iota((SEG, SEG + LANES), 0) < ones_col) | (ones_col >= SEG)).astype(f32).astype(bf16)
    lower = (iota((BINS, BINS), 1) < iota((BINS, BINS), 0)).astype(f32).astype(bf16)
    base = jnp.zeros((BINS, LANES), f32)
    members, counts, totals = [], [], []
    for s in range(GS // SEG):
        member = (bin_of[:, s * SEG:(s + 1) * SEG] == iota((BINS, SEG), 0)).astype(f32)
        both = dot(member.astype(bf16), upper)
        members.append(member)
        counts.append(both[:, :SEG])
        totals.append(both[:, SEG:])
        base = base + dot(lower, both[:, SEG:].astype(bf16))
    places = []
    for s in range(GS // SEG):
        offset = jnp.concatenate([base] * (SEG // LANES), 1)
        places.append(jnp.sum(members[s] * (counts[s] + offset), axis=0, keepdims=True))
        base = base + totals[s]
    place = jnp.concatenate(places, 1).astype(i32)
    slot = iota((1, GS), 1)
    row = iota((16, GS), 0)
    digit = jnp.where(row < 8, slot // 32, slot % 32).astype(f32)
    left = jnp.where((place // LANES) == (row % 8), digit, 0.0).astype(bf16)
    within = jnp.where(live, place % LANES, -1)
    right = (within == iota((LANES, GS), 0)).astype(f32).astype(bf16)
    both = dot(left, right, ((1,), (1,)))
    slots = (both[:8] * 32.0 + both[8:]).astype(i32)
    return place, slots


def gather(values, index):
    index = jnp.broadcast_to(index, (8, LANES))
    lane = index % LANES
    tile = index // LANES
    out = jnp.take_along_axis(values[:, :LANES], lane, axis=1)
    for k in range(1, CHUNKS):
        part = jnp.take_along_axis(values[:, k * LANES:(k + 1) * LANES], lane, axis=1)
        out = jnp.where(tile == k, part, out)
    return out


def split(v):
    high = v.astype(bf16)
    return high, (v - high.astype(f32)).astype(bf16)


def local_kernel(
    me_ref, scnt_ref, tcnt_ref, src_ref, tgt_ref,
    splace_ref, tplace_ref, w1_ref, mf_ref, mw_ref, sums_ref,
    rows_ref, vf_ref, vw_ref, lane_ref, tlane_ref, w2_ref, wins_v, wins_s, sem,
):
    own = tgt_ref.shape[1] // GS
    total = own + 2 * HALO

    def clear(g, _):
        rows_ref[pl.ds(pl.multiple_of(g * ROW_STRIDE + GS, 8), WIN), :] = jnp.zeros((WIN, LANES), f32)
        vf_ref[:, pl.ds(pl.multiple_of(g * VAL_STRIDE + GS, LANES), 384)] = jnp.zeros((F, 384), f32)
        vw_ref[:, pl.ds(pl.multiple_of(g * VAL_STRIDE + GS, LANES), 384)] = jnp.zeros((F, 384), f32)
        return 0

    lax.fori_loop(0, total, clear, 0)

    def sort_source(g, _):
        at = pl.multiple_of(g * GS, GS)
        live = slot_mask(scnt_ref, g)
        count = live_total(scnt_ref, g)
        points = src_ref[8:16, pl.ds(at, GS)]
        field = src_ref[0:8, pl.ds(at, GS)]
        place, slots = order(points[1:2], live)
        splace_ref[:, pl.ds(at, GS)] = place
        for h in range(CHUNKS):
            index = slots[h:h + 1]
            here = (iota((8, LANES), 1) + h * LANES) < count
            moved = gather(points, index)
            lane_ref[:, pl.ds(at + h * LANES, LANES)] = moved
            wide = jnp.concatenate([moved, jnp.zeros((LANES - 8, LANES), f32)], 0)
            rows_ref[pl.ds(pl.multiple_of(g * ROW_STRIDE + h * LANES, 8), LANES), :] = wide.T
            vf_ref[:, pl.ds(pl.multiple_of(g * VAL_STRIDE + h * LANES, LANES), LANES)] = jnp.where(
                here, gather(field, index), 0.0
            )
        return 0

    lax.fori_loop(0, total, sort_source, 0)

    def sort_target(g, _):
        at = pl.multiple_of(g * GS, GS)
        live = slot_mask(tcnt_ref, g)
        points = tgt_ref[:, pl.ds(at, GS)]
        place, slots = order(points[1:2], live)
        tplace_ref[:, pl.ds(at, GS)] = place
        for h in range(CHUNKS):
            tlane_ref[:, pl.ds(at + h * LANES, LANES)] = gather(points, slots[h:h + 1])
        return 0

    lax.fori_loop(0, own, sort_target, 0)

    def windows(points_ref, at, count, g, acc, column):
        place = iota((8, LANES), 1) + iota((8, LANES), 0) * LANES
        y = jnp.concatenate(
            [points_ref[1:2, pl.ds(at + h * LANES, LANES)] for h in range(CHUNKS)], 0
        )
        low = jnp.min(jnp.where(place < count, y, jnp.inf), axis=1, keepdims=True) - R
        high = jnp.max(jnp.where(place < count, y, -jnp.inf), axis=1, keepdims=True) + R
        packed = jnp.zeros((8, 1), i32)
        steps = jnp.zeros((8, 1), i32)
        for b in range(3):
            there = g + b - 1
            yq = lane_ref[1:2, pl.ds(pl.multiple_of(there * GS, GS), GS)]
            n = live_total(scnt_ref, there)
            slot = jnp.broadcast_to(iota((1, GS), 1), (8, GS))
            near = (yq >= low) & (yq <= high) & (slot < n)
            slot = slot.astype(f32)
            first = jnp.min(jnp.where(near, slot, 4096.0), axis=1, keepdims=True).astype(i32)
            end = jnp.max(jnp.where(near, slot + 1.0, 0.0), axis=1, keepdims=True).astype(i32)
            unit = jnp.where(end > 0, first // 16, 0)
            packed = packed + unit * (128 ** b)
            steps = jnp.maximum(steps, (end - unit * 16 + WIN - 1) // WIN)
        packed = packed + steps * (128 ** 3)
        return jnp.where(iota((8, LANES), 1) == column, packed, acc)

    def source_windows(g, acc):
        return windows(lane_ref, pl.multiple_of(g * GS, GS), live_total(scnt_ref, g), g, acc, g)

    def target_windows(g, acc):
        return windows(
            tlane_ref, pl.multiple_of(g * GS, GS), live_total(tcnt_ref, g), g + HALO, acc, g + total
        )

    acc = lax.fori_loop(1, total - 1, source_windows, jnp.zeros((8, LANES), i32))
    wins_v[...] = lax.fori_loop(0, own, target_windows, acc)
    copy = pltpu.make_async_copy(wins_v, wins_s, sem)
    copy.start()
    copy.wait()

    def interact(points, packed, k, g, value_refs):
        acc = None
        for b in range(3):
            there = g + b - 1
            start = pl.multiple_of(jnp.minimum(((packed >> (7 * b)) & 127) * 16 + k * WIN, GS), 16)
            rows = rows_ref[pl.ds(pl.multiple_of(there * ROW_STRIDE + start, 16), WIN), :]
            square = None
            for axis in range(3):
                offset = rows[:, axis:axis + 1] - points[axis:axis + 1, :]
                square = offset * offset if axis == 0 else square + offset * offset
            square = jnp.minimum(jnp.maximum(square, 1e-30), float(R * R))
            distance = square * lax.rsqrt(square)
            rest = R - distance
            rest = rest * rest
            phi = rest * rest * (distance + 1.0)
            high, low = split(phi)
            parts = []
            for ref in value_refs:
                window = ref[:, pl.ds(pl.multiple_of(there * VAL_STRIDE + start // LANES * LANES, LANES), 384)]
                window = pltpu.roll(window, lax.rem(384 - start % LANES, 384), 1)[:, :WIN]
                parts += list(split(window))
            left = jnp.concatenate(parts, 0)
            term = dot(left, high) + dot(left, low)
            acc = term if acc is None else acc + term
        return acc

    def pass_over(column0, g0, groups, points_ref, cnt_ref, value_refs, store):
        rows_out = 2 * F * len(value_refs)

        def chunk(i, _):
            g = i // CHUNKS
            c = i % CHUNKS
            at = pl.multiple_of(i * LANES, LANES)
            packed = wins_s[c, g + column0]
            points = points_ref[:, pl.ds(at, LANES)]

            def step(k, acc):
                return acc + interact(points, packed, k, g + g0, value_refs)

            acc = lax.fori_loop(0, packed >> 21, step, jnp.zeros((rows_out, LANES), f32))
            here = (iota((F, LANES), 1) + c * LANES) < live_total(cnt_ref, g)
            for v in range(len(value_refs)):
                out = (acc[16 * v:16 * v + 8] + acc[16 * v + 8:16 * v + 16]) * (1.0 / 256.0)
                store(v, g, c, at, jnp.where(here, out, 0.0))
            return 0

        lax.fori_loop(groups[0] * CHUNKS, groups[1] * CHUNKS, chunk, 0)

    def store_w1(v, g, c, at, out):
        vw_ref[:, pl.ds(pl.multiple_of(g * VAL_STRIDE + c * LANES, LANES), LANES)] = out

    for g in (0, total - 1):
        vw_ref[:, g * VAL_STRIDE:g * VAL_STRIDE + GS] = jnp.zeros((F, GS), f32)
    pass_over(0, 0, (1, total - 1), lane_ref, scnt_ref, [vf_ref], store_w1)

    def store_w2(v, g, c, at, out):
        w2_ref[:, pl.ds(pl.multiple_of(at - HALO * GS, LANES), LANES)] = out

    pass_over(0, 0, (HALO, total - HALO), lane_ref, scnt_ref, [vw_ref], store_w2)

    def store_mapped(v, g, c, at, out):
        (mf_ref, mw_ref)[v][:, pl.ds(at, LANES)] = out

    pass_over(total, HALO, (0, own), tlane_ref, tcnt_ref, [vf_ref, vw_ref], store_mapped)

    def first_sums(g, acc):
        ff, fw = acc
        at = pl.multiple_of((g + HALO) * VAL_STRIDE, LANES)
        f = vf_ref[:, pl.ds(at, GS)]
        w = vw_ref[:, pl.ds(at, GS)]
        w1_ref[:, pl.ds(pl.multiple_of(g * GS, GS), GS)] = w
        return ff + f * f, fw + f * w

    zero = jnp.zeros((F, GS), f32)
    ff, fw = lax.fori_loop(0, own, first_sums, (zero, zero))
    ff = jnp.sum(ff, axis=1, keepdims=True)
    fw = jnp.sum(fw, axis=1, keepdims=True)
    shift = jnp.where(ff > 0, fw / jnp.where(ff > 0, ff, 1.0), 0.0)

    def second_sums(g, acc):
        ee, ez, fz = acc
        at = pl.multiple_of((g + HALO) * VAL_STRIDE, LANES)
        f = vf_ref[:, pl.ds(at, GS)]
        w = vw_ref[:, pl.ds(at, GS)]
        e = w - shift * f
        z = w2_ref[:, pl.ds(pl.multiple_of(g * GS, GS), GS)] - shift * w
        return ee + e * e, ez + e * z, fz + f * z

    sums = lax.fori_loop(0, own, second_sums, (zero, zero, zero))
    sums = [ff, shift] + [jnp.sum(s, axis=1, keepdims=True) for s in sums]
    mine = iota((F, LANES), 1) == me_ref[0]
    for n, value in enumerate(sums):
        sums_ref[n * F:(n + 1) * F, :] = jnp.where(mine, value, 0.0)


def final_kernel(
    scnt_ref, tcnt_ref, sums_ref, rhs_ref, splace_ref, tplace_ref, w1_ref, mf_ref, mw_ref, coef_ref, mapped_ref
):
    own = rhs_ref.shape[1] // GS
    ff, shift, ee, ez, fz = (sums_ref[n * F:(n + 1) * F, :] for n in range(5))

    def over(x):
        return jnp.sum(x, axis=1, keepdims=True)

    total = over(ff)
    mean = over(ff * shift) / total
    delta = shift - mean
    e_e = over(ee + delta * delta * ff)
    e_ae = over(ez + delta * (ee + fz) + delta * delta * shift * ff)
    alpha0 = 1.0 / mean
    ratio = e_e / total
    beta = alpha0 * alpha0 * ratio
    alpha1 = e_e / (e_ae - alpha0 * ratio * e_e)
    c1 = -alpha1 * alpha0
    c0 = alpha0 + alpha1 * (1.0 + beta)

    def group(g, _):
        at = pl.multiple_of(g * GS, GS)
        w = w1_ref[:, pl.ds(at, GS)]
        m = c0 * mf_ref[:, pl.ds(at, GS)] + c1 * mw_ref[:, pl.ds(at, GS)]
        f = rhs_ref[:, pl.ds(at, GS)]
        splace = splace_ref[:, pl.ds(pl.multiple_of(at + HALO * GS, GS), GS)]
        tplace = tplace_ref[:, pl.ds(at, GS)]
        slive = slot_mask(scnt_ref, g)
        tlive = slot_mask(tcnt_ref, g)
        for h in range(CHUNKS):
            lanes = slice(h * LANES, (h + 1) * LANES)
            coef = c0 * f[:, lanes] + c1 * gather(w, splace[:, lanes])
            coef_ref[:, pl.ds(at + h * LANES, LANES)] = jnp.where(slive[:, lanes], coef, 0.0)
            out = gather(m, tplace[:, lanes])
            mapped_ref[:, pl.ds(at + h * LANES, LANES)] = jnp.where(tlive[:, lanes], out, 0.0)
        return 0

    lax.fori_loop(0, own, group, 0)


def run_local(me, scnt, tcnt, src, tgt):
    points = tgt.shape[1]
    total = points // GS + 2 * HALO
    vmem = pl.BlockSpec(memory_space=pltpu.VMEM)
    smem = pl.BlockSpec(memory_space=pltpu.SMEM)
    return pl.pallas_call(
        local_kernel,
        out_shape=[
            jax.ShapeDtypeStruct((1, total * GS), i32),
            jax.ShapeDtypeStruct((1, points), i32),
            jax.ShapeDtypeStruct((F, points), f32),
            jax.ShapeDtypeStruct((F, points), f32),
            jax.ShapeDtypeStruct((F, points), f32),
            jax.ShapeDtypeStruct((5 * F, LANES), f32),
        ],
        in_specs=[smem, smem, smem, vmem, vmem],
        out_specs=[vmem] * 6,
        scratch_shapes=[
            pltpu.VMEM((total * ROW_STRIDE, LANES), f32),
            pltpu.VMEM((F, total * VAL_STRIDE), f32),
            pltpu.VMEM((F, total * VAL_STRIDE), f32),
            pltpu.VMEM((8, total * GS), f32),
            pltpu.VMEM((8, points), f32),
            pltpu.VMEM((F, points), f32),
            pltpu.VMEM((8, LANES), i32),
            pltpu.SMEM((8, LANES), i32),
            pltpu.SemaphoreType.DMA,
        ],
        compiler_params=pltpu.CompilerParams(vmem_limit_bytes=56 * 1024 * 1024),
        name="local",
    )(me, scnt, tcnt, src, tgt)


def run_final(scnt, tcnt, sums, rhs, splace, tplace, w1, mf, mw):
    vmem = pl.BlockSpec(memory_space=pltpu.VMEM)
    smem = pl.BlockSpec(memory_space=pltpu.SMEM)
    return pl.pallas_call(
        final_kernel,
        out_shape=[jax.ShapeDtypeStruct(rhs.shape, f32)] * 2,
        in_specs=[smem, smem] + [vmem] * 7,
        out_specs=[vmem] * 2,
        compiler_params=pltpu.CompilerParams(vmem_limit_bytes=40 * 1024 * 1024),
        name="final",
    )(scnt, tcnt, sums, rhs, splace, tplace, w1, mf, mw)


def shifted(x, by):
    peers = lax.axis_size(AXES)
    pairs = [(i, i + by) for i in range(peers) if 0 <= i + by < peers]
    return lax.ppermute(x, AXES, pairs)


def on_device(src_points, tgt_points, src_count, tgt_count, pair_list, pair_total, rhs):
    reach = HALO * GS
    blocks = HALO * R
    own = jnp.concatenate([rhs, src_points, jnp.zeros((5, rhs.shape[1]), f32)], 0)
    before = shifted(own[:11, -reach:], 1)
    after = shifted(own[:11, :reach], -1)
    pad = ((0, 5), (0, 0))
    src = jnp.concatenate([jnp.pad(before, pad), own, jnp.pad(after, pad)], 1)
    scnt = jnp.concatenate([shifted(src_count[-blocks:], 1), src_count, shifted(src_count[:blocks], -1)])
    tgt = jnp.pad(tgt_points, ((0, 5), (0, 0)))
    me = lax.axis_index(AXES).astype(i32)[None]
    splace, tplace, w1, mf, mw, sums = run_local(me, scnt, tgt_count, src, tgt)
    sums = lax.psum(sums, AXES)
    return run_final(src_count, tgt_count, sums, rhs, splace, tplace, w1, mf, mw)


def solution(mesh):
    return jax.shard_map(
        on_device,
        mesh=mesh,
        in_specs=(
            P(None, AXES),
            P(None, AXES),
            P(AXES),
            P(AXES),
            P(None, AXES),
            P(AXES),
            P(None, AXES),
        ),
        out_specs=(P(None, AXES), P(None, AXES)),
        check_vma=False,
    )
```

```python
import functools

import jax
import jax.numpy as jnp
from jax import lax
from jax.experimental import pallas as pl
from jax.experimental.pallas import tpu as pltpu
from jax.sharding import PartitionSpec as P

R = 4
BP = 256
F = 8
GS = R * BP
HALO = 2
LANES = 128
CHUNKS = GS // LANES
BINS = 128
WIN = 192
ROW_STRIDE = GS + WIN
VAL_STRIDE = GS + 384
SEG = 256
BATCH = 4
AXES = ("src", "tgt")
f32 = jnp.float32
bf16 = jnp.bfloat16
i32 = jnp.int32


def iota(shape, dim):
    return lax.broadcasted_iota(i32, shape, dim)


def dot(a, b, dims=((1,), (0,))):
    return lax.dot_general(a, b, (dims, ((), ())), preferred_element_type=f32)


def slot_mask(cnt_ref, group):
    slot = iota((1, GS), 1)
    block = slot // BP
    limit = jnp.zeros((1, GS), i32)
    for k in range(R):
        limit = jnp.where(block == k, cnt_ref[group * R + k], limit)
    return (slot % BP) < limit


def live_total(cnt_ref, group):
    total = cnt_ref[group * R]
    for k in range(1, R):
        total = total + cnt_ref[group * R + k]
    return total


def order(y, live):
    low = jnp.min(jnp.where(live, y, jnp.inf))
    high = jnp.max(jnp.where(live, y, -jnp.inf))
    scale = BINS / jnp.maximum(high - low, 1e-30)
    scaled = jnp.minimum(jnp.maximum((y - low) * scale, 0.0), BINS - 1.0)
    bin_of = jnp.where(live, scaled.astype(i32), BINS)
    ones_col = iota((SEG, SEG + LANES), 1)
    upper = ((iota((SEG, SEG + LANES), 0) < ones_col) | (ones_col >= SEG)).astype(f32).astype(bf16)
    lower = (iota((BINS, BINS), 1) < iota((BINS, BINS), 0)).astype(f32).astype(bf16)
    base = jnp.zeros((BINS, LANES), f32)
    members, counts, totals = [], [], []
    for s in range(GS // SEG):
        member = (bin_of[:, s * SEG:(s + 1) * SEG] == iota((BINS, SEG), 0)).astype(f32)
        both = dot(member.astype(bf16), upper)
        members.append(member)
        counts.append(both[:, :SEG])
        totals.append(both[:, SEG:])
        base = base + dot(lower, both[:, SEG:].astype(bf16))
    places = []
    for s in range(GS // SEG):
        offset = jnp.concatenate([base] * (SEG // LANES), 1)
        places.append(jnp.sum(members[s] * (counts[s] + offset), axis=0, keepdims=True))
        base = base + totals[s]
    place = jnp.concatenate(places, 1).astype(i32)
    slot = iota((1, GS), 1)
    row = iota((16, GS), 0)
    digit = jnp.where(row < 8, slot // 32, slot % 32).astype(f32)
    left = jnp.where((place // LANES) == (row % 8), digit, 0.0).astype(bf16)
    within = jnp.where(live, place % LANES, -1)
    right = (within == iota((LANES, GS), 0)).astype(f32).astype(bf16)
    both = dot(left, right, ((1,), (1,)))
    slots = (both[:8] * 32.0 + both[8:]).astype(i32)
    return place, slots


def gather(values, index):
    index = jnp.broadcast_to(index, (8, LANES))
    lane = index % LANES
    tile = index // LANES
    out = jnp.take_along_axis(values[:, :LANES], lane, axis=1)
    for k in range(1, CHUNKS):
        part = jnp.take_along_axis(values[:, k * LANES:(k + 1) * LANES], lane, axis=1)
        out = jnp.where(tile == k, part, out)
    return out


def split(v):
    high = v.astype(bf16)
    return high, (v - high.astype(f32)).astype(bf16)


def local_kernel(
    scnt_ref, tcnt_ref, before_ref, after_ref, rhs_ref, points_ref, tgt_ref,
    splace_ref, tplace_ref, w1_ref, mf_ref, mw_ref, sums_ref,
    src_ref, rows_ref, vf_ref, vw_ref, lane_ref, tlane_ref, w2_ref, wins_v, wins_s, list_s, sem,
):
    own = tgt_ref.shape[1] // GS
    total = own + 2 * HALO

    reach = HALO * GS
    points = tgt_ref.shape[1]
    for at, refs in ((0, (before_ref,)), (reach, (rhs_ref, points_ref)), (reach + points, (after_ref,))):
        row = 0
        for ref in refs:
            src_ref[row:row + min(ref.shape[0], 11), at:at + ref.shape[1]] = ref[:11, :]
            row += ref.shape[0]

    def clear(g, _):
        rows_ref[:, pl.ds(pl.multiple_of(g * ROW_STRIDE + GS, 8), WIN), :] = jnp.zeros((3, WIN, LANES), f32)
        vf_ref[:, pl.ds(pl.multiple_of(g * VAL_STRIDE + GS, LANES), 384)] = jnp.zeros((F, 384), f32)
        vw_ref[:, pl.ds(pl.multiple_of(g * VAL_STRIDE, LANES), VAL_STRIDE)] = jnp.zeros((F, VAL_STRIDE), f32)
        return 0

    lax.fori_loop(0, total, clear, 0)
    w2_ref[...] = jnp.zeros_like(w2_ref)
    mf_ref[...] = jnp.zeros_like(mf_ref)
    mw_ref[...] = jnp.zeros_like(mw_ref)

    def sort_source(g, _):
        at = pl.multiple_of(g * GS, GS)
        live = slot_mask(scnt_ref, g)
        count = live_total(scnt_ref, g)
        points = jnp.concatenate([src_ref[8:11, pl.ds(at, GS)], jnp.zeros((5, GS), f32)], 0)
        field = src_ref[0:8, pl.ds(at, GS)]
        place, slots = order(points[1:2], live)
        splace_ref[:, pl.ds(at, GS)] = place
        for h in range(CHUNKS):
            index = slots[h:h + 1]
            here = (iota((8, LANES), 1) + h * LANES) < count
            moved = gather(points, index)
            lane_ref[:, pl.ds(at + h * LANES, LANES)] = moved
            wide = jnp.concatenate([moved, jnp.zeros((LANES - 8, LANES), f32)], 0)
            wide = wide.T
            row = pl.multiple_of(g * ROW_STRIDE + h * LANES, 8)
            for axis in range(3):
                rows_ref[axis, pl.ds(row, LANES), :] = jnp.broadcast_to(wide[:, axis:axis + 1], (LANES, LANES))
            vf_ref[:, pl.ds(pl.multiple_of(g * VAL_STRIDE + h * LANES, LANES), LANES)] = jnp.where(
                here, gather(field, index), 0.0
            )
        return 0

    lax.fori_loop(0, total, sort_source, 0)

    def sort_target(g, _):
        at = pl.multiple_of(g * GS, GS)
        live = slot_mask(tcnt_ref, g)
        points = jnp.concatenate([tgt_ref[:, pl.ds(at, GS)], jnp.zeros((5, GS), f32)], 0)
        place, slots = order(points[1:2], live)
        tplace_ref[:, pl.ds(at, GS)] = place
        for h in range(CHUNKS):
            tlane_ref[:, pl.ds(at + h * LANES, LANES)] = gather(points, slots[h:h + 1])
        return 0

    lax.fori_loop(0, own, sort_target, 0)

    def windows(points_ref, at, count, g, acc, column):
        place = iota((8, LANES), 1) + iota((8, LANES), 0) * LANES
        y = jnp.concatenate(
            [points_ref[1:2, pl.ds(at + h * LANES, LANES)] for h in range(CHUNKS)], 0
        )
        low = jnp.min(jnp.where(place < count, y, jnp.inf), axis=1, keepdims=True) - R
        high = jnp.max(jnp.where(place < count, y, -jnp.inf), axis=1, keepdims=True) + R
        packed = jnp.zeros((8, 1), i32)
        steps = jnp.zeros((8, 1), i32)
        for b in range(3):
            there = g + b - 1
            yq = lane_ref[1:2, pl.ds(pl.multiple_of(there * GS, GS), GS)]
            n = live_total(scnt_ref, there)
            slot = jnp.broadcast_to(iota((1, GS), 1), (8, GS))
            near = (yq >= low) & (yq <= high) & (slot < n)
            slot = slot.astype(f32)
            first = jnp.min(jnp.where(near, slot, 4096.0), axis=1, keepdims=True).astype(i32)
            end = jnp.max(jnp.where(near, slot + 1.0, 0.0), axis=1, keepdims=True).astype(i32)
            unit = jnp.where(end > 0, first // 16, 0)
            packed = packed + unit * (128 ** b)
            steps = jnp.maximum(steps, (end - unit * 16 + WIN - 1) // WIN)
        packed = packed + steps * (128 ** 3)
        return jnp.where(iota((8, LANES), 1) == column, packed, acc)

    def source_windows(g, acc):
        return windows(lane_ref, pl.multiple_of(g * GS, GS), live_total(scnt_ref, g), g, acc, g)

    def target_windows(g, acc):
        return windows(
            tlane_ref, pl.multiple_of(g * GS, GS), live_total(tcnt_ref, g), g + HALO, acc, g + total
        )

    acc = lax.fori_loop(1, total - 1, source_windows, jnp.zeros((8, LANES), i32))
    wins_v[...] = lax.fori_loop(0, own, target_windows, acc)
    copy = pltpu.make_async_copy(wins_v, wins_s, sem)
    copy.start()
    copy.wait()

    def interact(points, packed, k, g, value_refs):
        acc = None
        for b in range(3):
            there = g + b - 1
            start = pl.multiple_of(jnp.minimum(((packed >> (7 * b)) & 127) * 16 + k * WIN, GS), 16)
            row = pl.multiple_of(there * ROW_STRIDE + start, 16)
            square = None
            for axis in range(3):
                offset = rows_ref[axis, pl.ds(row, WIN), :] - points[axis:axis + 1, :]
                square = offset * offset if axis == 0 else square + offset * offset
            square = jnp.minimum(jnp.maximum(square, 1e-30), float(R * R))
            distance = square * lax.rsqrt(square)
            rest = R - distance
            rest = rest * rest
            phi = rest * rest * (distance + 1.0)
            high, low = split(phi)
            parts = []
            for ref in value_refs:
                window = ref[:, pl.ds(pl.multiple_of(there * VAL_STRIDE + start // LANES * LANES, LANES), 384)]
                window = pltpu.roll(window, lax.rem(384 - start % LANES, 384), 1)[:, :WIN]
                parts += list(split(window))
            left = jnp.concatenate(parts, 0)
            term = dot(left, jnp.concatenate([high, low], 1))
            acc = term if acc is None else acc + term
        return acc[:, :LANES] + acc[:, LANES:]

    def pass_over(column0, g0, groups, points_ref, cnt_ref, value_refs, store):
        rows_out = 2 * F * len(value_refs)

        def list_group(g, n):
            def list_chunk(c, n):
                list_s[n] = g * CHUNKS + c
                return n + 1

            return lax.fori_loop(0, (live_total(cnt_ref, g) + LANES - 1) // LANES, list_chunk, n)

        n = lax.fori_loop(groups[0], groups[1], list_group, 0)

        def batch(i, _):
            work = []
            for u in range(BATCH):
                item = list_s[jnp.minimum(i * BATCH + u, n - 1)]
                g = item // CHUNKS
                c = item % CHUNKS
                at = pl.multiple_of(item * LANES, LANES)
                packed = wins_s[c, g + column0]
                work.append((g, c, at, packed, points_ref[:, pl.ds(at, LANES)]))
            accs = tuple(interact(points, packed, 0, g + g0, value_refs) for g, c, at, packed, points in work)
            most = functools.reduce(jnp.maximum, [w[3] >> 21 for w in work])

            def step(k, accs):
                return tuple(
                    acc + interact(points, packed, k, g + g0, value_refs)
                    for acc, (g, c, at, packed, points) in zip(accs, work)
                )

            accs = lax.fori_loop(1, most, step, accs)
            for acc, (g, c, at, packed, points) in zip(accs, work):
                here = (iota((F, LANES), 1) + c * LANES) < live_total(cnt_ref, g)
                for v in range(len(value_refs)):
                    out = (acc[16 * v:16 * v + 8] + acc[16 * v + 8:16 * v + 16]) * (1.0 / 256.0)
                    store(v, g, c, at, jnp.where(here, out, 0.0))
            return 0

        lax.fori_loop(0, (n + BATCH - 1) // BATCH, batch, 0)

    def store_w1(v, g, c, at, out):
        vw_ref[:, pl.ds(pl.multiple_of(g * VAL_STRIDE + c * LANES, LANES), LANES)] = out

    pass_over(0, 0, (1, total - 1), lane_ref, scnt_ref, [vf_ref], store_w1)

    def store_w2(v, g, c, at, out):
        w2_ref[:, pl.ds(pl.multiple_of(at - HALO * GS, LANES), LANES)] = out

    pass_over(0, 0, (HALO, total - HALO), lane_ref, scnt_ref, [vw_ref], store_w2)

    def store_mapped(v, g, c, at, out):
        (mf_ref, mw_ref)[v][:, pl.ds(at, LANES)] = out

    pass_over(total, HALO, (0, own), tlane_ref, tcnt_ref, [vf_ref, vw_ref], store_mapped)

    def first_sums(g, acc):
        ff, fw = acc
        at = pl.multiple_of((g + HALO) * VAL_STRIDE, LANES)
        f = vf_ref[:, pl.ds(at, GS)]
        w = vw_ref[:, pl.ds(at, GS)]
        w1_ref[:, pl.ds(pl.multiple_of(g * GS, GS), GS)] = w
        return ff + f * f, fw + f * w

    zero = jnp.zeros((F, GS), f32)
    ff, fw = lax.fori_loop(0, own, first_sums, (zero, zero))
    ff = jnp.sum(ff, axis=1, keepdims=True)
    fw = jnp.sum(fw, axis=1, keepdims=True)
    shift = jnp.where(ff > 0, fw / jnp.where(ff > 0, ff, 1.0), 0.0)

    def second_sums(g, acc):
        ee, ez, fz = acc
        at = pl.multiple_of((g + HALO) * VAL_STRIDE, LANES)
        f = vf_ref[:, pl.ds(at, GS)]
        w = vw_ref[:, pl.ds(at, GS)]
        e = w - shift * f
        z = w2_ref[:, pl.ds(pl.multiple_of(g * GS, GS), GS)] - shift * w
        return ee + e * e, ez + e * z, fz + f * z

    sums = lax.fori_loop(0, own, second_sums, (zero, zero, zero))
    sums = [ff, shift] + [jnp.sum(s, axis=1, keepdims=True) for s in sums]
    tile = jnp.zeros((F, LANES), f32)
    for n, value in enumerate(sums):
        tile = jnp.where(iota((F, LANES), 1) == n, value, tile)
    sums_ref[...] = jnp.concatenate([tile, jnp.zeros((LANES - F, LANES), f32)], 0).T[:8]


def merge(tiles):
    ff, shift, ee, ez, fz = (tiles[:, n, :] for n in range(5))

    def over(x):
        return jnp.sum(x, axis=0, keepdims=True)

    total = over(ff)
    mean = over(ff * shift) / jnp.where(total > 0, total, 1.0)
    delta = shift - mean
    fw = shift * ff
    return [
        total,
        mean,
        over(ee + delta * delta * ff),
        over(ez + delta * (ee + fz) + delta * delta * fw),
        over(fz + delta * fw),
    ]


def share_kernel(sums_ref, out_ref, first, second, send1, recv1, send2, recv2):
    me = [lax.axis_index(name) for name in AXES]
    sizes = (second.shape[0], first.shape[0])

    def peer(axis, by):
        return {AXES[axis]: lax.rem(me[axis] + by, sizes[axis])}

    barrier = pltpu.get_barrier_semaphore()
    for axis in (0, 1):
        for by in range(1, sizes[axis]):
            pl.semaphore_signal(
                barrier, inc=1, device_id=peer(axis, by), device_id_type=pl.DeviceIdType.MESH
            )
    pl.semaphore_wait(barrier, sizes[0] + sizes[1] - 2)

    def exchange(axis, slots, send, recv):
        copies = []
        for by in range(1, sizes[axis]):
            copy = pltpu.make_async_remote_copy(
                src_ref=slots.at[0],
                dst_ref=slots.at[by],
                send_sem=send.at[by],
                recv_sem=recv.at[by],
                device_id=peer(axis, by),
                device_id_type=pl.DeviceIdType.MESH,
            )
            copy.start()
            copies.append(copy)
        for copy in copies:
            copy.wait()

    first[0] = sums_ref[...]
    exchange(1, first, send1, recv1)
    part = merge(first[...])
    second[0] = jnp.concatenate(part + [jnp.zeros((3, LANES), f32)], 0)
    exchange(0, second, send2, recv2)
    total, mean, e_e, e_ae, _ = merge(second[...])
    alpha0 = 1.0 / mean
    ratio = e_e / total
    beta = alpha0 * alpha0 * ratio
    alpha1 = e_e / (e_ae - alpha0 * ratio * e_e)
    c1 = -alpha1 * alpha0
    c0 = alpha0 + alpha1 * (1.0 + beta)
    out_ref[...] = jnp.concatenate([c0, c1, jnp.zeros((LANES - 2, LANES), f32)], 0).T[:F]


def final_kernel(
    scnt_ref, tcnt_ref, scale_ref, rhs_hbm, splace_hbm, tplace_hbm, w1_hbm, mf_hbm, mw_hbm,
    coef_ref, mapped_ref,
    rhs_ref, splace_ref, tplace_ref, w1_ref, mf_ref, mw_ref, sems,
):
    copies = [
        pltpu.make_async_copy(here, there, sems.at[n])
        for n, (here, there) in enumerate([
            (rhs_hbm, rhs_ref), (splace_hbm, splace_ref), (tplace_hbm, tplace_ref),
            (w1_hbm, w1_ref), (mf_hbm, mf_ref), (mw_hbm, mw_ref),
        ])
    ]
    for copy in copies:
        copy.start()
    for copy in copies:
        copy.wait()
    own = rhs_ref.shape[1] // GS
    c0 = scale_ref[:, 0:1]
    c1 = scale_ref[:, 1:2]

    def group(g, _):
        at = pl.multiple_of(g * GS, GS)
        w = w1_ref[:, pl.ds(at, GS)]
        m = c0 * mf_ref[:, pl.ds(at, GS)] + c1 * mw_ref[:, pl.ds(at, GS)]
        f = rhs_ref[:, pl.ds(at, GS)]
        splace = splace_ref[:, pl.ds(pl.multiple_of(at + HALO * GS, GS), GS)]
        tplace = tplace_ref[:, pl.ds(at, GS)]
        slive = slot_mask(scnt_ref, g)
        tlive = slot_mask(tcnt_ref, g)
        for h in range(CHUNKS):
            lanes = slice(h * LANES, (h + 1) * LANES)
            coef = c0 * f[:, lanes] + c1 * gather(w, splace[:, lanes])
            coef_ref[:, pl.ds(at + h * LANES, LANES)] = jnp.where(slive[:, lanes], coef, 0.0)
            out = gather(m, tplace[:, lanes])
            mapped_ref[:, pl.ds(at + h * LANES, LANES)] = jnp.where(tlive[:, lanes], out, 0.0)
        return 0

    lax.fori_loop(0, own, group, 0)


def run_local(scnt, tcnt, before, after, rhs, src, tgt):
    points = tgt.shape[1]
    total = points // GS + 2 * HALO
    vmem = pl.BlockSpec(memory_space=pltpu.VMEM)
    smem = pl.BlockSpec(memory_space=pltpu.SMEM)
    return pl.pallas_call(
        local_kernel,
        out_shape=[
            jax.ShapeDtypeStruct((1, total * GS), i32),
            jax.ShapeDtypeStruct((1, points), i32),
            jax.ShapeDtypeStruct((F, points), f32),
            jax.ShapeDtypeStruct((F, points), f32),
            jax.ShapeDtypeStruct((F, points), f32),
            jax.ShapeDtypeStruct((8, LANES), f32),
        ],
        in_specs=[smem, smem] + [vmem] * 5,
        out_specs=[vmem] * 6,
        scratch_shapes=[
            pltpu.VMEM((16, total * GS), f32),
            pltpu.VMEM((3, total * ROW_STRIDE, LANES), f32),
            pltpu.VMEM((F, total * VAL_STRIDE), f32),
            pltpu.VMEM((F, total * VAL_STRIDE), f32),
            pltpu.VMEM((8, total * GS), f32),
            pltpu.VMEM((8, points), f32),
            pltpu.VMEM((F, points), f32),
            pltpu.VMEM((8, LANES), i32),
            pltpu.SMEM((8, LANES), i32),
            pltpu.SMEM((total * CHUNKS,), i32),
            pltpu.SemaphoreType.DMA,
        ],
        compiler_params=pltpu.CompilerParams(vmem_limit_bytes=56 * 1024 * 1024),
        name="local",
    )(scnt, tcnt, before, after, rhs, src, tgt)


def run_share(sums, sizes):
    vmem = pl.BlockSpec(memory_space=pltpu.VMEM)
    return pl.pallas_call(
        share_kernel,
        out_shape=jax.ShapeDtypeStruct((F, LANES), f32),
        in_specs=[vmem],
        out_specs=vmem,
        scratch_shapes=[
            pltpu.VMEM((sizes[1], 8, LANES), f32),
            pltpu.VMEM((sizes[0], 8, LANES), f32),
            pltpu.SemaphoreType.DMA((sizes[1],)),
            pltpu.SemaphoreType.DMA((sizes[1],)),
            pltpu.SemaphoreType.DMA((sizes[0],)),
            pltpu.SemaphoreType.DMA((sizes[0],)),
        ],
        compiler_params=pltpu.CompilerParams(collective_id=1, has_side_effects=True),
        name="share",
    )(sums)


def run_final(scnt, tcnt, scale, *arrays):
    vmem = pl.BlockSpec(memory_space=pltpu.VMEM)
    smem = pl.BlockSpec(memory_space=pltpu.SMEM)
    anywhere = pl.BlockSpec(memory_space=pl.ANY)
    return pl.pallas_call(
        final_kernel,
        out_shape=[jax.ShapeDtypeStruct(arrays[0].shape, f32)] * 2,
        in_specs=[smem, smem, vmem] + [anywhere] * len(arrays),
        out_specs=[vmem] * 2,
        scratch_shapes=[pltpu.VMEM(a.shape, a.dtype) for a in arrays]
        + [pltpu.SemaphoreType.DMA((len(arrays),))],
        compiler_params=pltpu.CompilerParams(vmem_limit_bytes=60 * 1024 * 1024),
        name="final",
    )(scnt, tcnt, scale, *arrays)


def shifted(x, by):
    peers = lax.axis_size(AXES)
    pairs = [(i, i + by) for i in range(peers) if 0 <= i + by < peers]
    return lax.ppermute(x, AXES, pairs)


def on_device(src_points, tgt_points, src_count, tgt_count, pair_list, pair_total, rhs):
    reach = HALO * GS
    blocks = HALO * R
    counts = src_count.astype(f32)
    edges = [
        jnp.concatenate([rhs[:, part], src_points[:, part], jnp.pad(counts[rows], (0, reach - blocks))[None]], 0)
        for part, rows in ((slice(-reach, None), slice(-blocks, None)), (slice(0, reach), slice(0, blocks)))
    ]
    before = shifted(edges[0], 1)
    after = shifted(edges[1], -1)
    scnt = jnp.concatenate([before[11, :blocks].astype(i32), src_count, after[11, :blocks].astype(i32)])
    splace, tplace, w1, mf, mw, sums = run_local(scnt, tgt_count, before, after, rhs, src_points, tgt_points)
    scale = run_share(sums, [lax.axis_size(name) for name in AXES])
    return run_final(src_count, tgt_count, scale, rhs, splace, tplace, w1, mf, mw)


def solution(mesh):
    return jax.shard_map(
        on_device,
        mesh=mesh,
        in_specs=(
            P(None, AXES),
            P(None, AXES),
            P(AXES),
            P(AXES),
            P(None, AXES),
            P(AXES),
            P(None, AXES),
        ),
        out_specs=(P(None, AXES), P(None, AXES)),
        check_vma=False,
    )
```

```python
import jax
import jax.numpy as jnp
from jax import lax
from jax.experimental import pallas as pl
from jax.experimental.pallas import tpu as pltpu
from jax.sharding import PartitionSpec as P

R = 4
BP = 256
F = 8
GS = R * BP
HALO = 2
LANES = 128
CHUNKS = GS // LANES
BINS = 128
WIN = 192
MORE = 64
ROW_STRIDE = GS + WIN
VAL_STRIDE = GS + 384
SEG = 256
BATCH = 4
LAG = -(-15 // BATCH) + 1
TOGETHER = 4
AXES = ("src", "tgt")
f32 = jnp.float32
bf16 = jnp.bfloat16
i32 = jnp.int32


def iota(shape, dim):
    return lax.broadcasted_iota(i32, shape, dim)


def dot(a, b, dims=((1,), (0,))):
    return lax.dot_general(a, b, (dims, ((), ())), preferred_element_type=f32)


def slot_mask(cnt_ref, group):
    slot = iota((1, GS), 1)
    block = slot // BP
    limit = jnp.zeros((1, GS), i32)
    for k in range(R):
        limit = jnp.where(block == k, cnt_ref[group * R + k], limit)
    return (slot % BP) < limit


def live_total(cnt_ref, group):
    total = cnt_ref[group * R]
    for k in range(1, R):
        total = total + cnt_ref[group * R + k]
    return total


def order(y, live, upper, lower):
    low = jnp.min(jnp.where(live, y, jnp.inf), axis=1, keepdims=True)
    high = jnp.max(jnp.where(live, y, -jnp.inf), axis=1, keepdims=True)
    scale = BINS / jnp.maximum(high - low, 1e-30)
    scaled = jnp.minimum(jnp.maximum((y - low) * scale, 0.0), BINS - 1.0)
    bin_of = jnp.where(live, scaled.astype(i32), BINS)
    base = jnp.zeros((BINS, LANES), f32)
    members, counts, totals = [], [], []
    for s in range(GS // SEG):
        member = (bin_of[:, s * SEG:(s + 1) * SEG] == iota((BINS, SEG), 0)).astype(f32)
        both = dot(member.astype(bf16), upper[...])
        members.append(member)
        counts.append(both[:, :SEG])
        totals.append(both[:, SEG:])
        base = base + dot(lower[...], both[:, SEG:].astype(bf16))
    places = []
    for s in range(GS // SEG):
        offset = jnp.concatenate([base] * (SEG // LANES), 1)
        places.append(jnp.sum(members[s] * (counts[s] + offset), axis=0, keepdims=True))
        base = base + totals[s]
    place = jnp.concatenate(places, 1).astype(i32)
    within = jnp.where(live, place % LANES, -1)
    to_lane = (within == iota((LANES, GS), 0)).astype(f32).astype(bf16)
    return place, to_lane


def in_order(values, place, to_lane):
    n = values.shape[0]
    first = (values * 0.99609375).astype(bf16)
    rest = values - first.astype(f32)
    second = rest.astype(bf16)
    rest = rest - second.astype(f32)
    parts = jnp.concatenate([first.astype(f32), second.astype(f32), rest] + [jnp.zeros_like(rest)] * (n // 8 % 2), 0)
    parts = parts.astype(bf16)
    rows = parts.shape[0]
    chunk = jnp.broadcast_to(place // LANES, (16, GS))
    left = []
    for h in range(CHUNKS):
        here = jnp.where(chunk == h, 1.0, 0.0).astype(bf16)
        left += [parts[r:r + 16] * here for r in range(0, rows, 16)]
    moved = dot(jnp.concatenate(left, 0), to_lane, ((1,), (1,)))
    pieces = []
    for h in range(CHUNKS):
        a, b, c = (moved[h * rows + k * n:h * rows + (k + 1) * n] for k in range(3))
        pieces.append(a + b + c)
    return pieces


def gather(values, index):
    index = jnp.broadcast_to(index, (8, LANES))
    lane = index % LANES
    tile = index // LANES
    out = jnp.take_along_axis(values[:, :LANES], lane, axis=1)
    for k in range(1, CHUNKS):
        part = jnp.take_along_axis(values[:, k * LANES:(k + 1) * LANES], lane, axis=1)
        out = jnp.where(tile == k, part, out)
    return out


def split(v):
    high = v.astype(bf16)
    return high, (v - high.astype(f32)).astype(bf16)


def local_kernel(
    scnt_ref, tcnt_ref, before_ref, after_ref, rhs_ref, points_ref, tgt_ref,
    splace_ref, tplace_ref, w1_ref, mf_ref, mw_ref, sums_ref,
    src_ref, rows_ref, vf_ref, vw_ref, lane_ref, tlane_ref, w2_ref, cache_ref, wins_v, wins_s, list_s, upper_ref, lower_ref, sem,
):
    own = tgt_ref.shape[1] // GS
    total = own + 2 * HALO

    reach = HALO * GS
    points = tgt_ref.shape[1]
    for at, refs in ((0, (before_ref,)), (reach, (rhs_ref, points_ref)), (reach + points, (after_ref,))):
        row = 0
        for ref in refs:
            src_ref[row:row + min(ref.shape[0], 11), at:at + ref.shape[1]] = ref[:11, :]
            row += ref.shape[0]

    src_ref[11:16, :] = jnp.zeros((5, src_ref.shape[1]), f32)

    def clear(g, _):
        rows_ref[:, pl.ds(pl.multiple_of(g * ROW_STRIDE + GS, 8), WIN), :] = jnp.zeros((3, WIN, LANES), f32)
        vf_ref[:, pl.ds(pl.multiple_of(g * VAL_STRIDE + GS, LANES), 384)] = jnp.zeros((F, 384), f32)
        vw_ref[:, pl.ds(pl.multiple_of(g * VAL_STRIDE, LANES), VAL_STRIDE)] = jnp.zeros((F, VAL_STRIDE), f32)
        return 0

    lax.fori_loop(0, total, clear, 0)
    w2_ref[...] = jnp.zeros_like(w2_ref)
    mf_ref[...] = jnp.zeros_like(mf_ref)
    mw_ref[...] = jnp.zeros_like(mw_ref)

    ones_col = iota((SEG, SEG + LANES), 1)
    upper_ref[...] = ((iota((SEG, SEG + LANES), 0) < ones_col) | (ones_col >= SEG)).astype(f32).astype(bf16)
    lower_ref[...] = (iota((BINS, BINS), 1) < iota((BINS, BINS), 0)).astype(f32).astype(bf16)

    def sort_source(g):
        at = pl.multiple_of(g * GS, GS)
        live = slot_mask(scnt_ref, g)
        values = src_ref[:, pl.ds(at, GS)]
        place, to_lane = order(values[9:10], live, upper_ref, lower_ref)
        splace_ref[:, pl.ds(at, GS)] = place
        for h, moved in enumerate(in_order(values, place, to_lane)):
            points = moved[8:]
            lane_ref[:, pl.ds(at + h * LANES, LANES)] = points
            wide = jnp.concatenate([points, jnp.zeros((LANES - 8, LANES), f32)], 0).T
            row = pl.multiple_of(g * ROW_STRIDE + h * LANES, 8)
            for axis in range(3):
                rows_ref[axis, pl.ds(row, LANES), :] = jnp.broadcast_to(wide[:, axis:axis + 1], (LANES, LANES))
            vf_ref[:, pl.ds(pl.multiple_of(g * VAL_STRIDE + h * LANES, LANES), LANES)] = moved[:8]

    def sort_target(g):
        at = pl.multiple_of(g * GS, GS)
        live = slot_mask(tcnt_ref, g)
        points = jnp.concatenate([tgt_ref[:, pl.ds(at, GS)], jnp.zeros((5, GS), f32)], 0)
        place, to_lane = order(points[1:2], live, upper_ref, lower_ref)
        tplace_ref[:, pl.ds(at, GS)] = place
        for h, moved in enumerate(in_order(points, place, to_lane)):
            tlane_ref[:, pl.ds(at + h * LANES, LANES)] = moved

    def several(fn, n):
        def some(i, _):
            for u in range(TOGETHER):
                fn(TOGETHER * i + u)
            return 0

        lax.fori_loop(0, n // TOGETHER, some, 0)

    several(sort_source, total)
    several(sort_target, own)

    def windows(points_ref, at, count, g, acc, column):
        place = iota((8, LANES), 1) + iota((8, LANES), 0) * LANES
        y = jnp.concatenate(
            [points_ref[1:2, pl.ds(at + h * LANES, LANES)] for h in range(CHUNKS)], 0
        )
        low = jnp.min(jnp.where(place < count, y, jnp.inf), axis=1, keepdims=True) - R
        high = jnp.max(jnp.where(place < count, y, -jnp.inf), axis=1, keepdims=True) + R
        packed = jnp.zeros((8, 1), i32)
        steps = jnp.zeros((8, 1), i32)
        for b in range(3):
            there = g + b - 1
            yq = lane_ref[1:2, pl.ds(pl.multiple_of(there * GS, GS), GS)]
            n = live_total(scnt_ref, there)
            slot = jnp.broadcast_to(iota((1, GS), 1), (8, GS))
            near = (yq >= low) & (yq <= high) & (slot < n)
            slot = slot.astype(f32)
            first = jnp.min(jnp.where(near, slot, 4096.0), axis=1, keepdims=True).astype(i32)
            end = jnp.max(jnp.where(near, slot + 1.0, 0.0), axis=1, keepdims=True).astype(i32)
            unit = jnp.where(end > 0, first // 16, 0)
            packed = packed + unit * (128 ** b)
            steps = jnp.maximum(steps, (end - unit * 16 - WIN + MORE - 1) // MORE)
        packed = packed + steps * (128 ** 3)
        return jnp.where(iota((8, LANES), 1) == column, packed, acc)

    def source_windows(g, acc):
        return windows(lane_ref, pl.multiple_of(g * GS, GS), live_total(scnt_ref, g), g, acc, g)

    def target_windows(g, acc):
        return windows(
            tlane_ref, pl.multiple_of(g * GS, GS), live_total(tcnt_ref, g), g + HALO, acc, g + total
        )

    acc = lax.fori_loop(1, total - 1, source_windows, jnp.zeros((8, LANES), i32))
    wins_v[...] = lax.fori_loop(0, own, target_windows, acc)
    copy = pltpu.make_async_copy(wins_v, wins_s, sem)
    copy.start()
    copy.wait()

    def window_start(packed, b, skip):
        return pl.multiple_of(jnp.minimum(((packed >> (7 * b)) & 127) * 16 + skip, GS), 16)

    def near_phi(points, there, start, width):
        row = pl.multiple_of(there * ROW_STRIDE + start, 16)
        square = None
        for axis in range(3):
            offset = rows_ref[axis, pl.ds(row, width), :] - points[axis:axis + 1, :]
            square = offset * offset if axis == 0 else square + offset * offset
        square = jnp.minimum(jnp.maximum(square, 1e-30), float(R * R))
        distance = square * lax.rsqrt(square)
        rest = R - distance
        rest = rest * rest
        return jnp.concatenate(split(rest * rest * (distance + 1.0)), 1)

    def near_values(value_refs, there, start, width):
        parts = []
        for ref in value_refs:
            window = ref[:, pl.ds(pl.multiple_of(there * VAL_STRIDE + start // LANES * LANES, LANES), 384)]
            window = pltpu.roll(window, lax.rem(384 - start % LANES, 384), 1)[:, :width]
            parts += list(split(window))
        return jnp.concatenate(parts, 0)

    def interact(points, packed, skip, width, g, value_refs, keep=None, kept=None):
        acc = None
        for b in range(3):
            start = window_start(packed, b, skip)
            if kept is None:
                phi = near_phi(points, g + b - 1, start, width)
            else:
                phi = cache_ref[kept, b * WIN:(b + 1) * WIN, :]
            if keep is not None:
                cache_ref[keep, b * WIN:(b + 1) * WIN, :] = phi
            term = dot(near_values(value_refs, g + b - 1, start, width), phi)
            acc = term if acc is None else acc + term
        return acc[:, :LANES] + acc[:, LANES:]

    def list_chunks(cnt_ref, first, end):
        def list_group(g, n):
            def list_chunk(c, n):
                list_s[n] = g * CHUNKS + c
                return n + 1

            return lax.fori_loop(0, (live_total(cnt_ref, g) + LANES - 1) // LANES, list_chunk, n)

        return lax.fori_loop(first, end, list_group, 0)

    def work_on(i, n, column0, g0, points_ref, cnt_ref, value_refs, store, keep=False, kept=False):
        work = []
        for u in range(BATCH):
            item = list_s[jnp.minimum(i * BATCH + u, n - 1)]
            g = item // CHUNKS
            c = item % CHUNKS
            at = pl.multiple_of(item * LANES, LANES)
            packed = wins_s[c, g + column0]
            slot = lax.rem(i, LAG + 1) * BATCH + u
            work.append((g, c, at, packed, points_ref[:, pl.ds(at, LANES)], slot))
        accs = tuple(
            interact(
                points, packed, 0, WIN, g + g0, value_refs, slot if keep else None, slot if kept else None
            )
            for g, c, at, packed, points, slot in work
        )
        for acc, (g, c, at, packed, points, slot) in zip(accs, work):

            def more(k, acc, g=g, packed=packed, points=points):
                return acc + interact(points, packed, WIN + k * MORE, MORE, g + g0, value_refs)

            acc = lax.fori_loop(0, packed >> 21, more, acc)
            here = (iota((F, LANES), 1) + c * LANES) < live_total(cnt_ref, g)
            for v in range(len(value_refs)):
                out = (acc[16 * v:16 * v + 8] + acc[16 * v + 8:16 * v + 16]) * (1.0 / 256.0)
                store(v, g, c, at, jnp.where(here, out, 0.0))

    def store_w1(v, g, c, at, out):
        vw_ref[:, pl.ds(pl.multiple_of(g * VAL_STRIDE + c * LANES, LANES), LANES)] = out

    def store_w2(v, g, c, at, out):
        w2_ref[:, pl.ds(at, LANES)] = out

    n = list_chunks(scnt_ref, 1, total - 1)
    batches = (n + BATCH - 1) // BATCH

    def first_pass(i):
        work_on(i, n, 0, 0, lane_ref, scnt_ref, [vf_ref], store_w1, keep=True)

    def second_pass(i):
        work_on(i, n, 0, 0, lane_ref, scnt_ref, [vw_ref], store_w2, kept=True)

    def lead(i, _):
        first_pass(i)
        return 0

    def both(i, _):
        second_pass(i - LAG)
        first_pass(i)
        return 0

    def trail(i, _):
        second_pass(i - LAG)
        return 0

    lax.fori_loop(0, LAG, lead, 0)
    lax.fori_loop(LAG, batches, both, 0)
    lax.fori_loop(jnp.maximum(batches, LAG), batches + LAG, trail, 0)

    def store_mapped(v, g, c, at, out):
        (mf_ref, mw_ref)[v][:, pl.ds(at, LANES)] = out

    n = list_chunks(tcnt_ref, 0, own)

    def mapped_pass(i, _):
        work_on(i, n, total, HALO, tlane_ref, tcnt_ref, [vf_ref, vw_ref], store_mapped)
        return 0

    lax.fori_loop(0, (n + BATCH - 1) // BATCH, mapped_pass, 0)

    def first_sums(g, acc):
        ff, fw = acc
        at = pl.multiple_of((g + HALO) * VAL_STRIDE, LANES)
        f = vf_ref[:, pl.ds(at, GS)]
        w = vw_ref[:, pl.ds(at, GS)]
        w1_ref[:, pl.ds(pl.multiple_of(g * GS, GS), GS)] = w
        return ff + f * f, fw + f * w

    zero = jnp.zeros((F, GS), f32)
    ff, fw = lax.fori_loop(0, own, first_sums, (zero, zero))
    ff = jnp.sum(ff, axis=1, keepdims=True)
    fw = jnp.sum(fw, axis=1, keepdims=True)
    shift = jnp.where(ff > 0, fw / jnp.where(ff > 0, ff, 1.0), 0.0)

    def second_sums(g, acc):
        ee, ez, fz = acc
        at = pl.multiple_of((g + HALO) * VAL_STRIDE, LANES)
        f = vf_ref[:, pl.ds(at, GS)]
        w = vw_ref[:, pl.ds(at, GS)]
        e = w - shift * f
        z = w2_ref[:, pl.ds(pl.multiple_of((g + HALO) * GS, GS), GS)] - shift * w
        return ee + e * e, ez + e * z, fz + f * z

    sums = lax.fori_loop(0, own, second_sums, (zero, zero, zero))
    sums = [ff, shift] + [jnp.sum(s, axis=1, keepdims=True) for s in sums]
    tile = jnp.zeros((F, LANES), f32)
    for n, value in enumerate(sums):
        tile = jnp.where(iota((F, LANES), 1) == n, value, tile)
    sums_ref[...] = jnp.concatenate([tile, jnp.zeros((LANES - F, LANES), f32)], 0).T[:8]


def merge(tiles):
    ff, shift, ee, ez, fz = (tiles[:, n, :] for n in range(5))

    def over(x):
        return jnp.sum(x, axis=0, keepdims=True)

    total = over(ff)
    mean = over(ff * shift) / jnp.where(total > 0, total, 1.0)
    delta = shift - mean
    fw = shift * ff
    return [
        total,
        mean,
        over(ee + delta * delta * ff),
        over(ez + delta * (ee + fz) + delta * delta * fw),
        over(fz + delta * fw),
    ]


def share_kernel(sums_ref, out_ref, first, second, send1, recv1, send2, recv2):
    me = [lax.axis_index(name) for name in AXES]
    sizes = (second.shape[0], first.shape[0])

    def peer(axis, by):
        return {AXES[axis]: lax.rem(me[axis] + by, sizes[axis])}

    barrier = pltpu.get_barrier_semaphore()
    for axis in (0, 1):
        for by in range(1, sizes[axis]):
            pl.semaphore_signal(
                barrier, inc=1, device_id=peer(axis, by), device_id_type=pl.DeviceIdType.MESH
            )
    pl.semaphore_wait(barrier, sizes[0] + sizes[1] - 2)

    def exchange(axis, slots, send, recv):
        copies = []
        for by in range(1, sizes[axis]):
            copy = pltpu.make_async_remote_copy(
                src_ref=slots.at[0],
                dst_ref=slots.at[by],
                send_sem=send.at[by],
                recv_sem=recv.at[by],
                device_id=peer(axis, by),
                device_id_type=pl.DeviceIdType.MESH,
            )
            copy.start()
            copies.append(copy)
        for copy in copies:
            copy.wait()

    first[0] = sums_ref[...]
    exchange(1, first, send1, recv1)
    part = merge(first[...])
    second[0] = jnp.concatenate(part + [jnp.zeros((3, LANES), f32)], 0)
    exchange(0, second, send2, recv2)
    total, mean, e_e, e_ae, _ = merge(second[...])
    alpha0 = 1.0 / mean
    ratio = e_e / total
    beta = alpha0 * alpha0 * ratio
    alpha1 = e_e / (e_ae - alpha0 * ratio * e_e)
    c1 = -alpha1 * alpha0
    c0 = alpha0 + alpha1 * (1.0 + beta)
    out_ref[...] = jnp.concatenate([c0, c1, jnp.zeros((LANES - 2, LANES), f32)], 0).T[:F]


def final_kernel(
    scnt_ref, tcnt_ref, scale_ref, rhs_hbm, splace_hbm, tplace_hbm, w1_hbm, mf_hbm, mw_hbm,
    coef_ref, mapped_ref,
    rhs_ref, splace_ref, tplace_ref, w1_ref, mf_ref, mw_ref, sems,
):
    copies = [
        pltpu.make_async_copy(here, there, sems.at[n])
        for n, (here, there) in enumerate([
            (rhs_hbm, rhs_ref), (splace_hbm, splace_ref), (tplace_hbm, tplace_ref),
            (w1_hbm, w1_ref), (mf_hbm, mf_ref), (mw_hbm, mw_ref),
        ])
    ]
    for copy in copies:
        copy.start()
    for copy in copies:
        copy.wait()
    own = rhs_ref.shape[1] // GS
    c0 = scale_ref[:, 0:1]
    c1 = scale_ref[:, 1:2]

    def group(g, _):
        at = pl.multiple_of(g * GS, GS)
        w = w1_ref[:, pl.ds(at, GS)]
        m = c0 * mf_ref[:, pl.ds(at, GS)] + c1 * mw_ref[:, pl.ds(at, GS)]
        f = rhs_ref[:, pl.ds(at, GS)]
        splace = splace_ref[:, pl.ds(pl.multiple_of(at + HALO * GS, GS), GS)]
        tplace = tplace_ref[:, pl.ds(at, GS)]
        slive = slot_mask(scnt_ref, g)
        tlive = slot_mask(tcnt_ref, g)
        for h in range(CHUNKS):
            lanes = slice(h * LANES, (h + 1) * LANES)
            coef = c0 * f[:, lanes] + c1 * gather(w, splace[:, lanes])
            coef_ref[:, pl.ds(at + h * LANES, LANES)] = jnp.where(slive[:, lanes], coef, 0.0)
            out = gather(m, tplace[:, lanes])
            mapped_ref[:, pl.ds(at + h * LANES, LANES)] = jnp.where(tlive[:, lanes], out, 0.0)
        return 0

    lax.fori_loop(0, own, group, 0)


def run_local(scnt, tcnt, before, after, rhs, src, tgt):
    points = tgt.shape[1]
    total = points // GS + 2 * HALO
    vmem = pl.BlockSpec(memory_space=pltpu.VMEM)
    smem = pl.BlockSpec(memory_space=pltpu.SMEM)
    return pl.pallas_call(
        local_kernel,
        out_shape=[
            jax.ShapeDtypeStruct((1, total * GS), i32),
            jax.ShapeDtypeStruct((1, points), i32),
            jax.ShapeDtypeStruct((F, points), f32),
            jax.ShapeDtypeStruct((F, points), f32),
            jax.ShapeDtypeStruct((F, points), f32),
            jax.ShapeDtypeStruct((8, LANES), f32),
        ],
        in_specs=[smem, smem] + [vmem] * 5,
        out_specs=[vmem] * 6,
        scratch_shapes=[
            pltpu.VMEM((16, total * GS), f32),
            pltpu.VMEM((3, total * ROW_STRIDE, LANES), f32),
            pltpu.VMEM((F, total * VAL_STRIDE), f32),
            pltpu.VMEM((F, total * VAL_STRIDE), f32),
            pltpu.VMEM((8, total * GS), f32),
            pltpu.VMEM((8, points), f32),
            pltpu.VMEM((F, total * GS), f32),
            pltpu.VMEM(((LAG + 1) * BATCH, 3 * WIN, 2 * LANES), bf16),
            pltpu.VMEM((8, LANES), i32),
            pltpu.SMEM((8, LANES), i32),
            pltpu.SMEM((total * CHUNKS,), i32),
            pltpu.VMEM((SEG, SEG + LANES), bf16),
            pltpu.VMEM((BINS, BINS), bf16),
            pltpu.SemaphoreType.DMA,
        ],
        compiler_params=pltpu.CompilerParams(vmem_limit_bytes=56 * 1024 * 1024),
        name="local",
    )(scnt, tcnt, before, after, rhs, src, tgt)


def run_share(sums, sizes):
    vmem = pl.BlockSpec(memory_space=pltpu.VMEM)
    return pl.pallas_call(
        share_kernel,
        out_shape=jax.ShapeDtypeStruct((F, LANES), f32),
        in_specs=[vmem],
        out_specs=vmem,
        scratch_shapes=[
            pltpu.VMEM((sizes[1], 8, LANES), f32),
            pltpu.VMEM((sizes[0], 8, LANES), f32),
            pltpu.SemaphoreType.DMA((sizes[1],)),
            pltpu.SemaphoreType.DMA((sizes[1],)),
            pltpu.SemaphoreType.DMA((sizes[0],)),
            pltpu.SemaphoreType.DMA((sizes[0],)),
        ],
        compiler_params=pltpu.CompilerParams(collective_id=1, has_side_effects=True),
        name="share",
    )(sums)


def run_final(scnt, tcnt, scale, *arrays):
    vmem = pl.BlockSpec(memory_space=pltpu.VMEM)
    smem = pl.BlockSpec(memory_space=pltpu.SMEM)
    anywhere = pl.BlockSpec(memory_space=pl.ANY)
    return pl.pallas_call(
        final_kernel,
        out_shape=[jax.ShapeDtypeStruct(arrays[0].shape, f32)] * 2,
        in_specs=[smem, smem, vmem] + [anywhere] * len(arrays),
        out_specs=[vmem] * 2,
        scratch_shapes=[pltpu.VMEM(a.shape, a.dtype) for a in arrays]
        + [pltpu.SemaphoreType.DMA((len(arrays),))],
        compiler_params=pltpu.CompilerParams(vmem_limit_bytes=60 * 1024 * 1024),
        name="final",
    )(scnt, tcnt, scale, *arrays)


def shifted(x, by):
    peers = lax.axis_size(AXES)
    pairs = [(i, i + by) for i in range(peers) if 0 <= i + by < peers]
    return lax.ppermute(x, AXES, pairs)


def on_device(src_points, tgt_points, src_count, tgt_count, pair_list, pair_total, rhs):
    reach = HALO * GS
    blocks = HALO * R
    counts = src_count.astype(f32)
    edges = [
        jnp.concatenate([rhs[:, part], src_points[:, part], jnp.pad(counts[rows], (0, reach - blocks))[None]], 0)
        for part, rows in ((slice(-reach, None), slice(-blocks, None)), (slice(0, reach), slice(0, blocks)))
    ]
    before = shifted(edges[0], 1)
    after = shifted(edges[1], -1)
    scnt = jnp.concatenate([before[11, :blocks].astype(i32), src_count, after[11, :blocks].astype(i32)])
    splace, tplace, w1, mf, mw, sums = run_local(scnt, tgt_count, before, after, rhs, src_points, tgt_points)
    scale = run_share(sums, [lax.axis_size(name) for name in AXES])
    return run_final(src_count, tgt_count, scale, rhs, splace, tplace, w1, mf, mw)


def solution(mesh):
    return jax.shard_map(
        on_device,
        mesh=mesh,
        in_specs=(
            P(None, AXES),
            P(None, AXES),
            P(AXES),
            P(AXES),
            P(None, AXES),
            P(AXES),
            P(None, AXES),
        ),
        out_specs=(P(None, AXES), P(None, AXES)),
        check_vma=False,
    )
```

```python
import jax
import jax.numpy as jnp
from jax import lax
from jax.experimental import pallas as pl
from jax.experimental.pallas import tpu as pltpu
from jax.sharding import PartitionSpec as P

R = 4
BP = 256
F = 8
GS = R * BP
HALO = 2
LANES = 128
CHUNKS = GS // LANES
BINS = 128
WINS = (208, 176, 208)
WIN_AT = (0, 208, 384)
MORE = 64
PIECE = 16
ROW_STRIDE = GS + max(WINS)
VAL_STRIDE = GS + 384
SEG = 256
BATCH = 4
LAG = -(-15 // BATCH) + 1
TOGETHER = 4
AXES = ("src", "tgt")
f32 = jnp.float32
bf16 = jnp.bfloat16
i32 = jnp.int32


def iota(shape, dim):
    return lax.broadcasted_iota(i32, shape, dim)


def dot(a, b, dims=((1,), (0,))):
    return lax.dot_general(a, b, (dims, ((), ())), preferred_element_type=f32)


def slot_mask(cnt_ref, group):
    slot = iota((1, GS), 1)
    block = slot // BP
    limit = jnp.zeros((1, GS), i32)
    for k in range(R):
        limit = jnp.where(block == k, cnt_ref[group * R + k], limit)
    return (slot % BP) < limit


def live_total(cnt_ref, group):
    total = cnt_ref[group * R]
    for k in range(1, R):
        total = total + cnt_ref[group * R + k]
    return total


def order(y, live, upper, lower):
    low = jnp.min(jnp.where(live, y, jnp.inf), axis=1, keepdims=True)
    high = jnp.max(jnp.where(live, y, -jnp.inf), axis=1, keepdims=True)
    scale = BINS / jnp.maximum(high - low, 1e-30)
    scaled = jnp.minimum(jnp.maximum((y - low) * scale, 0.0), BINS - 1.0)
    bin_of = jnp.where(live, scaled.astype(i32), BINS)
    members, counts = [], []
    for s in range(GS // SEG):
        member = (bin_of[:, s * SEG:(s + 1) * SEG] == iota((BINS, SEG), 0)).astype(f32)
        members.append(member)
        counts.append(dot(member.astype(bf16), upper[...]))
    totals = [c[:, -1:] + m[:, -1:] for c, m in zip(counts, members)]
    column = iota((BINS, LANES), 1)
    table = jnp.zeros((BINS, LANES), f32)
    for s, t in enumerate(totals):
        table = jnp.where(column == s, t, table)
    base = jnp.sum(dot(lower[...], table.astype(bf16)), axis=1, keepdims=True)
    places = []
    for m, c, t in zip(members, counts, totals):
        places.append(jnp.sum(m * (c + base), axis=0, keepdims=True))
        base = base + t
    place = jnp.concatenate(places, 1).astype(i32)
    within = jnp.where(live, place % LANES, -1)
    to_lane = (within == iota((LANES, GS), 0)).astype(f32).astype(bf16)
    return place, to_lane


def in_order(points, field, place, to_lane):
    first = (points * 0.99609375).astype(bf16).astype(f32)
    second = (points - first).astype(bf16).astype(f32)
    parts = [first, second, points - first - second, jnp.zeros((7, GS), f32)]
    if field is not None:
        high = field.astype(bf16).astype(f32)
        parts += [high, field - high]
    parts = jnp.concatenate(parts, 0).astype(bf16)
    rows = parts.shape[0]
    chunk = jnp.broadcast_to(place // LANES, (16, GS))
    left = []
    for h in range(CHUNKS):
        here = jnp.where(chunk == h, 1.0, 0.0).astype(bf16)
        left += [parts[r:r + 16] * here for r in range(0, rows, 16)]
    moved = dot(jnp.concatenate(left, 0), to_lane, ((1,), (1,)))
    pieces = []
    for h in range(CHUNKS):
        piece = moved[h * rows:(h + 1) * rows]
        points = piece[0:3] + piece[3:6] + piece[6:9]
        points = jnp.concatenate([points, jnp.zeros((5, LANES), f32)], 0)
        pieces.append((points, None if field is None else piece[16:24] + piece[24:32], piece[:16]))
    return pieces


def gather(values, index):
    index = jnp.broadcast_to(index, (8, LANES))
    lane = index % LANES
    tile = index // LANES
    out = jnp.take_along_axis(values[:, :LANES], lane, axis=1)
    for k in range(1, CHUNKS):
        part = jnp.take_along_axis(values[:, k * LANES:(k + 1) * LANES], lane, axis=1)
        out = jnp.where(tile == k, part, out)
    return out


def split(v):
    high = v.astype(bf16)
    return high, (v - high.astype(f32)).astype(bf16)


def local_kernel(
    scnt_ref, tcnt_ref, before_ref, after_ref, rhs_ref, points_ref, tgt_ref,
    splace_ref, tplace_ref, w1_ref, mf_ref, mw_ref, sums_ref,
    src_ref, rows_ref, vf_ref, vw_ref, lane_ref, tlane_ref, w2_ref, cache_ref, wins_v, wins_s, list_s, upper_ref, lower_ref, spread_ref, sem,
):
    own = tgt_ref.shape[1] // GS
    total = own + 2 * HALO

    reach = HALO * GS
    points = tgt_ref.shape[1]
    for at, refs in ((0, (before_ref,)), (reach, (rhs_ref, points_ref)), (reach + points, (after_ref,))):
        row = 0
        for ref in refs:
            src_ref[row:row + min(ref.shape[0], 11), at:at + ref.shape[1]] = ref[:11, :]
            row += ref.shape[0]

    src_ref[11:16, :] = jnp.zeros((5, src_ref.shape[1]), f32)

    def clear(g, _):
        rows_ref[:, pl.ds(pl.multiple_of(g * ROW_STRIDE + GS, 8), max(WINS)), :] = jnp.zeros(
            (3, max(WINS), LANES), f32
        )
        vf_ref[:, pl.ds(pl.multiple_of(g * VAL_STRIDE + GS, LANES), 384)] = jnp.zeros((F, 384), f32)
        vw_ref[:, pl.ds(pl.multiple_of(g * VAL_STRIDE, LANES), VAL_STRIDE)] = jnp.zeros((F, VAL_STRIDE), f32)
        return 0

    lax.fori_loop(0, total, clear, 0)
    w2_ref[...] = jnp.zeros_like(w2_ref)
    mf_ref[...] = jnp.zeros_like(mf_ref)
    mw_ref[...] = jnp.zeros_like(mw_ref)

    upper_ref[...] = (iota((SEG, SEG), 0) < iota((SEG, SEG), 1)).astype(f32).astype(bf16)
    lower_ref[...] = (iota((BINS, BINS), 1) < iota((BINS, BINS), 0)).astype(f32).astype(bf16)

    part = iota((16, 3 * LANES), 0)
    spread_ref[...] = ((part < 9) & (part % 3 == iota((16, 3 * LANES), 1) // LANES)).astype(f32).astype(bf16)

    def sort_source(g):
        at = pl.multiple_of(g * GS, GS)
        live = slot_mask(scnt_ref, g)
        values = src_ref[:, pl.ds(at, GS)]
        place, to_lane = order(values[9:10], live, upper_ref, lower_ref)
        splace_ref[:, pl.ds(at, GS)] = place
        pieces = in_order(values[8:11], values[:8], place, to_lane)
        for h, (points, field, _) in enumerate(pieces):
            lane_ref[:, pl.ds(at + h * LANES, LANES)] = points
            vf_ref[:, pl.ds(pl.multiple_of(g * VAL_STRIDE + h * LANES, LANES), LANES)] = field
        parts = jnp.concatenate([piece[2] for piece in pieces], 1).astype(bf16)
        wide = dot(parts, spread_ref[...], ((0,), (0,)))
        for axis in range(3):
            rows_ref[axis, pl.ds(pl.multiple_of(g * ROW_STRIDE, 8), GS), :] = wide[:, axis * LANES:(axis + 1) * LANES]

    def sort_target(g):
        at = pl.multiple_of(g * GS, GS)
        live = slot_mask(tcnt_ref, g)
        points = tgt_ref[:, pl.ds(at, GS)]
        place, to_lane = order(points[1:2], live, upper_ref, lower_ref)
        tplace_ref[:, pl.ds(at, GS)] = place
        for h, (moved, _, _) in enumerate(in_order(points, None, place, to_lane)):
            tlane_ref[:, pl.ds(at + h * LANES, LANES)] = moved

    def several(fn, n):
        def some(i, _):
            for u in range(TOGETHER):
                fn(TOGETHER * i + u)
            return 0

        lax.fori_loop(0, n // TOGETHER, some, 0)

    several(sort_source, total)
    several(sort_target, own)

    def windows(points_ref, at, count, g, acc, column):
        place = iota((8, LANES), 1) + iota((8, LANES), 0) * LANES
        y = jnp.concatenate(
            [points_ref[1:2, pl.ds(at + h * LANES, LANES)] for h in range(CHUNKS)], 0
        )
        low = jnp.min(jnp.where(place < count, y, jnp.inf), axis=1, keepdims=True) - R
        high = jnp.max(jnp.where(place < count, y, -jnp.inf), axis=1, keepdims=True) + R
        packed = jnp.zeros((8, 1), i32)
        steps = jnp.zeros((8, 1), i32)
        for b in range(3):
            there = g + b - 1
            yq = lane_ref[1:2, pl.ds(pl.multiple_of(there * GS, GS), GS)]
            n = live_total(scnt_ref, there)
            slot = jnp.broadcast_to(iota((1, GS), 1), (8, GS))
            near = (yq >= low) & (yq <= high) & (slot < n)
            slot = slot.astype(f32)
            first = jnp.min(jnp.where(near, slot, 4096.0), axis=1, keepdims=True).astype(i32)
            end = jnp.max(jnp.where(near, slot + 1.0, 0.0), axis=1, keepdims=True).astype(i32)
            unit = jnp.where(end > 0, first // 8, 0)
            packed = packed + unit * (128 ** b)
            steps = jnp.maximum(steps, (end - unit * 8 - WINS[b] + MORE - 1) // MORE)
        packed = packed + steps * (128 ** 3)
        return jnp.where(iota((8, LANES), 1) == column, packed, acc)

    def source_windows(g, acc):
        return windows(lane_ref, pl.multiple_of(g * GS, GS), live_total(scnt_ref, g), g, acc, g)

    def target_windows(g, acc):
        return windows(
            tlane_ref, pl.multiple_of(g * GS, GS), live_total(tcnt_ref, g), g + HALO, acc, g + total
        )

    def two(fn, first):
        return lambda i, acc: fn(first + 2 * i + 1, fn(first + 2 * i, acc))

    acc = lax.fori_loop(0, (total - 2) // 2, two(source_windows, 1), jnp.zeros((8, LANES), i32))
    wins_v[...] = lax.fori_loop(0, own // 2, two(target_windows, 0), acc)
    copy = pltpu.make_async_copy(wins_v, wins_s, sem)
    copy.start()
    copy.wait()

    def window_start(packed, b, skip):
        return pl.multiple_of(jnp.minimum(((packed >> (7 * b)) & 127) * 8 + skip, GS), 8)

    def near_phi(points, there, start, width):
        row = pl.multiple_of(there * ROW_STRIDE + start, 8)
        pieces = []
        for r in range(0, width, PIECE):
            square = None
            for axis in range(3):
                offset = rows_ref[axis, pl.ds(row + r, PIECE), :] - points[axis:axis + 1, :]
                square = offset * offset if axis == 0 else square + offset * offset
            square = jnp.minimum(jnp.maximum(square, 1e-30), float(R * R))
            distance = square * lax.rsqrt(square)
            rest = R - distance
            rest = rest * rest
            pieces.append(jnp.concatenate(split(rest * rest * (distance + 1.0)), 1))
        return jnp.concatenate(pieces, 0)

    def near_values(value_refs, there, start, width):
        parts = []
        for ref in value_refs:
            window = ref[:, pl.ds(pl.multiple_of(there * VAL_STRIDE + start // LANES * LANES, LANES), 384)]
            window = pltpu.roll(window, lax.rem(384 - start % LANES, 384), 1)[:, :width]
            parts += list(split(window))
        return jnp.concatenate(parts, 0)

    def interact(points, packed, skips, widths, g, value_refs, keep=None, kept=None):
        acc = None
        for b in range(3):
            width = widths[b]
            start = window_start(packed, b, skips[b])
            rows = slice(WIN_AT[b], WIN_AT[b] + width)
            if kept is None:
                phi = near_phi(points, g + b - 1, start, width)
            else:
                phi = cache_ref[kept, rows, :]
            if keep is not None:
                cache_ref[keep, rows, :] = phi
            term = dot(near_values(value_refs, g + b - 1, start, width), phi)
            acc = term if acc is None else acc + term
        return acc[:, :LANES] + acc[:, LANES:]

    def list_chunks(cnt_ref, first, end):
        def list_group(g, n):
            def list_chunk(c, n):
                list_s[n] = g * CHUNKS + c
                return n + 1

            return lax.fori_loop(0, (live_total(cnt_ref, g) + LANES - 1) // LANES, list_chunk, n)

        return lax.fori_loop(first, end, list_group, 0)

    def work_on(i, n, column0, g0, points_ref, cnt_ref, value_refs, place, keep=False, kept=False):
        work = []
        for u in range(BATCH):
            item = list_s[jnp.minimum(i * BATCH + u, n - 1)]
            g = item // CHUNKS
            c = item % CHUNKS
            at = pl.multiple_of(item * LANES, LANES)
            packed = wins_s[c, g + column0]
            slot = lax.rem(i, LAG + 1) * BATCH + u
            steps = jnp.where(i * BATCH + u < n, packed >> 21, 0)
            work.append((g, c, at, packed, points_ref[:, pl.ds(at, LANES)], slot, steps))
        accs = tuple(
            interact(
                points, packed, (0, 0, 0), WINS, g + g0, value_refs, slot if keep else None, slot if kept else None
            )
            for g, c, at, packed, points, slot, steps in work
        )

        def finish(acc, v, g, c):
            here = (iota((F, LANES), 1) + c * LANES) < live_total(cnt_ref, g)
            out = (acc[16 * v:16 * v + 8] + acc[16 * v + 8:16 * v + 16]) * (1.0 / 256.0)
            return jnp.where(here, out, 0.0)

        for acc, (g, c, at, packed, points, slot, steps) in zip(accs, work):
            for v in range(len(value_refs)):
                place(v, g, c, at)[...] = finish(acc, v, g, c)

        def rest():
            for g, c, at, packed, points, slot, steps in work:

                def more(k, _, g=g, c=c, at=at, packed=packed, points=points):
                    skips = [w + k * MORE for w in WINS]
                    acc = interact(points, packed, skips, (MORE,) * 3, g + g0, value_refs)
                    for v in range(len(value_refs)):
                        place(v, g, c, at)[...] += finish(acc, v, g, c)
                    return 0

                lax.fori_loop(0, steps, more, 0)

        return sum(w[-1] for w in work), rest

    def run_rest(*rests):
        @pl.when(sum(steps for steps, _ in rests) > 0)
        def _():
            for _, rest in rests:
                rest()

    def place_w1(v, g, c, at):
        return vw_ref.at[:, pl.ds(pl.multiple_of(g * VAL_STRIDE + c * LANES, LANES), LANES)]

    def place_w2(v, g, c, at):
        return w2_ref.at[:, pl.ds(at, LANES)]

    n = list_chunks(scnt_ref, 1, total - 1)
    batches = (n + BATCH - 1) // BATCH

    def first_pass(i):
        return work_on(i, n, 0, 0, lane_ref, scnt_ref, [vf_ref], place_w1, keep=True)

    def second_pass(i):
        return work_on(i, n, 0, 0, lane_ref, scnt_ref, [vw_ref], place_w2, kept=True)

    def lead(i, _):
        run_rest(first_pass(i))
        return 0

    def both(i, _):
        run_rest(second_pass(i - LAG), first_pass(i))
        return 0

    def trail(i, _):
        run_rest(second_pass(i - LAG))
        return 0

    lax.fori_loop(0, LAG, lead, 0)
    lax.fori_loop(LAG, batches, both, 0)
    lax.fori_loop(jnp.maximum(batches, LAG), batches + LAG, trail, 0)

    def place_mapped(v, g, c, at):
        return (mf_ref, mw_ref)[v].at[:, pl.ds(at, LANES)]

    n = list_chunks(tcnt_ref, 0, own)

    def mapped_pass(i, _):
        run_rest(work_on(i, n, total, HALO, tlane_ref, tcnt_ref, [vf_ref, vw_ref], place_mapped))
        return 0

    lax.fori_loop(0, (n + BATCH - 1) // BATCH, mapped_pass, 0)

    def first_sums(g, acc):
        ff, fw = acc
        at = pl.multiple_of((g + HALO) * VAL_STRIDE, LANES)
        f = vf_ref[:, pl.ds(at, GS)]
        w = vw_ref[:, pl.ds(at, GS)]
        w1_ref[:, pl.ds(pl.multiple_of(g * GS, GS), GS)] = w
        return ff + f * f, fw + f * w

    zero = jnp.zeros((F, GS), f32)
    ff, fw = lax.fori_loop(0, own, first_sums, (zero, zero))
    ff = jnp.sum(ff, axis=1, keepdims=True)
    fw = jnp.sum(fw, axis=1, keepdims=True)
    shift = jnp.where(ff > 0, fw / jnp.where(ff > 0, ff, 1.0), 0.0)

    def second_sums(g, acc):
        ee, ez, fz = acc
        at = pl.multiple_of((g + HALO) * VAL_STRIDE, LANES)
        f = vf_ref[:, pl.ds(at, GS)]
        w = vw_ref[:, pl.ds(at, GS)]
        e = w - shift * f
        z = w2_ref[:, pl.ds(pl.multiple_of((g + HALO) * GS, GS), GS)] - shift * w
        return ee + e * e, ez + e * z, fz + f * z

    sums = lax.fori_loop(0, own, second_sums, (zero, zero, zero))
    sums = [ff, shift] + [jnp.sum(s, axis=1, keepdims=True) for s in sums]
    tile = jnp.zeros((F, LANES), f32)
    for n, value in enumerate(sums):
        tile = jnp.where(iota((F, LANES), 1) == n, value, tile)
    sums_ref[...] = jnp.concatenate([tile, jnp.zeros((LANES - F, LANES), f32)], 0).T[:8]


def merge(tiles):
    ff, shift, ee, ez, fz = (tiles[:, n, :] for n in range(5))

    def over(x):
        return jnp.sum(x, axis=0, keepdims=True)

    total = over(ff)
    mean = over(ff * shift) / jnp.where(total > 0, total, 1.0)
    delta = shift - mean
    fw = shift * ff
    return [
        total,
        mean,
        over(ee + delta * delta * ff),
        over(ez + delta * (ee + fz) + delta * delta * fw),
        over(fz + delta * fw),
    ]


def share_kernel(sums_ref, out_ref, first, second, send1, recv1, send2, recv2):
    me = [lax.axis_index(name) for name in AXES]
    sizes = (second.shape[0], first.shape[0])

    def peer(axis, by):
        return {AXES[axis]: lax.rem(me[axis] + by, sizes[axis])}

    barrier = pltpu.get_barrier_semaphore()
    for axis in (0, 1):
        for by in range(1, sizes[axis]):
            pl.semaphore_signal(
                barrier, inc=1, device_id=peer(axis, by), device_id_type=pl.DeviceIdType.MESH
            )
    pl.semaphore_wait(barrier, sizes[0] + sizes[1] - 2)

    def exchange(axis, slots, send, recv):
        copies = []
        for by in range(1, sizes[axis]):
            copy = pltpu.make_async_remote_copy(
                src_ref=slots.at[0],
                dst_ref=slots.at[by],
                send_sem=send.at[by],
                recv_sem=recv.at[by],
                device_id=peer(axis, by),
                device_id_type=pl.DeviceIdType.MESH,
            )
            copy.start()
            copies.append(copy)
        for copy in copies:
            copy.wait()

    first[0] = sums_ref[...]
    exchange(1, first, send1, recv1)
    part = merge(first[...])
    second[0] = jnp.concatenate(part + [jnp.zeros((3, LANES), f32)], 0)
    exchange(0, second, send2, recv2)
    total, mean, e_e, e_ae, _ = merge(second[...])
    alpha0 = 1.0 / mean
    ratio = e_e / total
    beta = alpha0 * alpha0 * ratio
    alpha1 = e_e / (e_ae - alpha0 * ratio * e_e)
    c1 = -alpha1 * alpha0
    c0 = alpha0 + alpha1 * (1.0 + beta)
    out_ref[...] = jnp.concatenate([c0, c1, jnp.zeros((LANES - 2, LANES), f32)], 0).T[:F]


def final_kernel(
    scnt_ref, tcnt_ref, scale_ref, rhs_hbm, splace_hbm, tplace_hbm, w1_hbm, mf_hbm, mw_hbm,
    coef_ref, mapped_ref,
    rhs_ref, splace_ref, tplace_ref, w1_ref, mf_ref, mw_ref, sems,
):
    copies = [
        pltpu.make_async_copy(here, there, sems.at[n])
        for n, (here, there) in enumerate([
            (rhs_hbm, rhs_ref), (splace_hbm, splace_ref), (tplace_hbm, tplace_ref),
            (w1_hbm, w1_ref), (mf_hbm, mf_ref), (mw_hbm, mw_ref),
        ])
    ]
    for copy in copies:
        copy.start()
    for copy in copies:
        copy.wait()
    own = rhs_ref.shape[1] // GS
    c0 = scale_ref[:, 0:1]
    c1 = scale_ref[:, 1:2]

    def group(g, _):
        at = pl.multiple_of(g * GS, GS)
        w = w1_ref[:, pl.ds(at, GS)]
        m = c0 * mf_ref[:, pl.ds(at, GS)] + c1 * mw_ref[:, pl.ds(at, GS)]
        f = rhs_ref[:, pl.ds(at, GS)]
        splace = splace_ref[:, pl.ds(pl.multiple_of(at + HALO * GS, GS), GS)]
        tplace = tplace_ref[:, pl.ds(at, GS)]
        slive = slot_mask(scnt_ref, g)
        tlive = slot_mask(tcnt_ref, g)
        for h in range(CHUNKS):
            lanes = slice(h * LANES, (h + 1) * LANES)
            coef = c0 * f[:, lanes] + c1 * gather(w, splace[:, lanes])
            coef_ref[:, pl.ds(at + h * LANES, LANES)] = jnp.where(slive[:, lanes], coef, 0.0)
            out = gather(m, tplace[:, lanes])
            mapped_ref[:, pl.ds(at + h * LANES, LANES)] = jnp.where(tlive[:, lanes], out, 0.0)
        return 0

    lax.fori_loop(0, own, group, 0)


def run_local(scnt, tcnt, before, after, rhs, src, tgt):
    points = tgt.shape[1]
    total = points // GS + 2 * HALO
    vmem = pl.BlockSpec(memory_space=pltpu.VMEM)
    smem = pl.BlockSpec(memory_space=pltpu.SMEM)
    return pl.pallas_call(
        local_kernel,
        out_shape=[
            jax.ShapeDtypeStruct((1, total * GS), i32),
            jax.ShapeDtypeStruct((1, points), i32),
            jax.ShapeDtypeStruct((F, points), f32),
            jax.ShapeDtypeStruct((F, points), f32),
            jax.ShapeDtypeStruct((F, points), f32),
            jax.ShapeDtypeStruct((8, LANES), f32),
        ],
        in_specs=[smem, smem] + [vmem] * 5,
        out_specs=[vmem] * 6,
        scratch_shapes=[
            pltpu.VMEM((16, total * GS), f32),
            pltpu.VMEM((3, total * ROW_STRIDE, LANES), f32),
            pltpu.VMEM((F, total * VAL_STRIDE), f32),
            pltpu.VMEM((F, total * VAL_STRIDE), f32),
            pltpu.VMEM((8, total * GS), f32),
            pltpu.VMEM((8, points), f32),
            pltpu.VMEM((F, total * GS), f32),
            pltpu.VMEM(((LAG + 1) * BATCH, sum(WINS), 2 * LANES), bf16),
            pltpu.VMEM((8, LANES), i32),
            pltpu.SMEM((8, LANES), i32),
            pltpu.SMEM((total * CHUNKS,), i32),
            pltpu.VMEM((SEG, SEG), bf16),
            pltpu.VMEM((BINS, BINS), bf16),
            pltpu.VMEM((16, 3 * LANES), bf16),
            pltpu.SemaphoreType.DMA,
        ],
        compiler_params=pltpu.CompilerParams(vmem_limit_bytes=56 * 1024 * 1024),
        name="local",
    )(scnt, tcnt, before, after, rhs, src, tgt)


def run_share(sums, sizes):
    vmem = pl.BlockSpec(memory_space=pltpu.VMEM)
    return pl.pallas_call(
        share_kernel,
        out_shape=jax.ShapeDtypeStruct((F, LANES), f32),
        in_specs=[vmem],
        out_specs=vmem,
        scratch_shapes=[
            pltpu.VMEM((sizes[1], 8, LANES), f32),
            pltpu.VMEM((sizes[0], 8, LANES), f32),
            pltpu.SemaphoreType.DMA((sizes[1],)),
            pltpu.SemaphoreType.DMA((sizes[1],)),
            pltpu.SemaphoreType.DMA((sizes[0],)),
            pltpu.SemaphoreType.DMA((sizes[0],)),
        ],
        compiler_params=pltpu.CompilerParams(collective_id=1, has_side_effects=True),
        name="share",
    )(sums)


def run_final(scnt, tcnt, scale, *arrays):
    vmem = pl.BlockSpec(memory_space=pltpu.VMEM)
    smem = pl.BlockSpec(memory_space=pltpu.SMEM)
    anywhere = pl.BlockSpec(memory_space=pl.ANY)
    return pl.pallas_call(
        final_kernel,
        out_shape=[jax.ShapeDtypeStruct(arrays[0].shape, f32)] * 2,
        in_specs=[smem, smem, vmem] + [anywhere] * len(arrays),
        out_specs=[vmem] * 2,
        scratch_shapes=[pltpu.VMEM(a.shape, a.dtype) for a in arrays]
        + [pltpu.SemaphoreType.DMA((len(arrays),))],
        compiler_params=pltpu.CompilerParams(vmem_limit_bytes=60 * 1024 * 1024),
        name="final",
    )(scnt, tcnt, scale, *arrays)


def shifted(x, by):
    peers = lax.axis_size(AXES)
    pairs = [(i, i + by) for i in range(peers) if 0 <= i + by < peers]
    return lax.ppermute(x, AXES, pairs)


def on_device(src_points, tgt_points, src_count, tgt_count, pair_list, pair_total, rhs):
    reach = HALO * GS
    blocks = HALO * R
    counts = src_count.astype(f32)
    edges = [
        jnp.concatenate([rhs[:, part], src_points[:, part], jnp.pad(counts[rows], (0, reach - blocks))[None]], 0)
        for part, rows in ((slice(-reach, None), slice(-blocks, None)), (slice(0, reach), slice(0, blocks)))
    ]
    before = shifted(edges[0], 1)
    after = shifted(edges[1], -1)
    scnt = jnp.concatenate([before[11, :blocks].astype(i32), src_count, after[11, :blocks].astype(i32)])
    splace, tplace, w1, mf, mw, sums = run_local(scnt, tgt_count, before, after, rhs, src_points, tgt_points)
    scale = run_share(sums, [lax.axis_size(name) for name in AXES])
    return run_final(src_count, tgt_count, scale, rhs, splace, tplace, w1, mf, mw)


def solution(mesh):
    return jax.shard_map(
        on_device,
        mesh=mesh,
        in_specs=(
            P(None, AXES),
            P(None, AXES),
            P(AXES),
            P(AXES),
            P(None, AXES),
            P(AXES),
            P(None, AXES),
        ),
        out_specs=(P(None, AXES), P(None, AXES)),
        check_vma=False,
    )
```

```python
import jax
import jax.numpy as jnp
from jax import lax
from jax.experimental import pallas as pl
from jax.experimental.pallas import tpu as pltpu
from jax.sharding import PartitionSpec as P

R = 4
BP = 256
F = 8
GS = R * BP
HALO = 2
LANES = 128
CHUNKS = GS // LANES
BINS = 128
WINS = (208, 176, 208)
WIN_AT = (0, 208, 384)
MORE = 64
PIECE = 16
ROW_STRIDE = GS + max(WINS)
VAL_STRIDE = GS + 384
SEG = 256
BATCH = 4
LAG = -(-15 // BATCH) + 1
TOGETHER = 4
AXES = ("src", "tgt")
f32 = jnp.float32
bf16 = jnp.bfloat16
i32 = jnp.int32


def iota(shape, dim):
    return lax.broadcasted_iota(i32, shape, dim)


def dot(a, b, dims=((1,), (0,))):
    return lax.dot_general(a, b, (dims, ((), ())), preferred_element_type=f32)


def slot_mask(cnt_ref, group):
    slot = iota((1, GS), 1)
    block = slot // BP
    limit = jnp.zeros((1, GS), i32)
    for k in range(R):
        limit = jnp.where(block == k, cnt_ref[group * R + k], limit)
    return (slot % BP) < limit


def live_total(cnt_ref, group):
    total = cnt_ref[group * R]
    for k in range(1, R):
        total = total + cnt_ref[group * R + k]
    return total


def order(y, live, upper, lower):
    low = jnp.min(jnp.where(live, y, jnp.inf), axis=1, keepdims=True)
    high = jnp.max(jnp.where(live, y, -jnp.inf), axis=1, keepdims=True)
    scale = BINS / jnp.maximum(high - low, 1e-30)
    scaled = jnp.minimum(jnp.maximum((y - low) * scale, 0.0), BINS - 1.0)
    bin_of = jnp.where(live, scaled.astype(i32), BINS)
    members, counts = [], []
    for s in range(GS // SEG):
        member = (bin_of[:, s * SEG:(s + 1) * SEG] == iota((BINS, SEG), 0)).astype(f32)
        members.append(member)
        counts.append(dot(member.astype(bf16), upper[...]))
    totals = [c[:, -1:] + m[:, -1:] for c, m in zip(counts, members)]
    column = iota((BINS, LANES), 1)
    table = jnp.zeros((BINS, LANES), f32)
    for s, t in enumerate(totals):
        table = jnp.where(column == s, t, table)
    base = jnp.sum(dot(lower[...], table.astype(bf16)), axis=1, keepdims=True)
    places = []
    for m, c, t in zip(members, counts, totals):
        places.append(jnp.sum(m * (c + base), axis=0, keepdims=True))
        base = base + t
    place = jnp.concatenate(places, 1).astype(i32)
    within = jnp.where(live, place % LANES, -1)
    to_lane = (within == iota((LANES, GS), 0)).astype(f32).astype(bf16)
    return place, to_lane


def in_order(points, field, place, to_lane):
    first = (points * 0.99609375).astype(bf16).astype(f32)
    second = (points - first).astype(bf16).astype(f32)
    parts = [first, second, points - first - second, jnp.zeros((7, GS), f32)]
    if field is not None:
        high = field.astype(bf16).astype(f32)
        parts += [high, field - high]
    parts = jnp.concatenate(parts, 0).astype(bf16)
    rows = parts.shape[0]
    chunk = jnp.broadcast_to(place // LANES, (16, GS))
    left = []
    for h in range(CHUNKS):
        here = jnp.where(chunk == h, 1.0, 0.0).astype(bf16)
        left += [parts[r:r + 16] * here for r in range(0, rows, 16)]
    moved = dot(jnp.concatenate(left, 0), to_lane, ((1,), (1,)))
    pieces = []
    for h in range(CHUNKS):
        piece = moved[h * rows:(h + 1) * rows]
        points = piece[0:3] + piece[3:6] + piece[6:9]
        points = jnp.concatenate([points, jnp.zeros((5, LANES), f32)], 0)
        pieces.append((points, None if field is None else piece[16:24] + piece[24:32], piece[:16]))
    return pieces


def gather(values, index):
    index = jnp.broadcast_to(index, (8, LANES))
    lane = index % LANES
    tile = index // LANES
    out = jnp.take_along_axis(values[:, :LANES], lane, axis=1)
    for k in range(1, CHUNKS):
        part = jnp.take_along_axis(values[:, k * LANES:(k + 1) * LANES], lane, axis=1)
        out = jnp.where(tile == k, part, out)
    return out


def split(v):
    high = v.astype(bf16)
    return high, (v - high.astype(f32)).astype(bf16)


def local_kernel(
    scnt_ref, tcnt_ref, bf_ref, bx_ref, af_ref, ax_ref, rhs_ref, points_ref, tgt_ref,
    splace_ref, tplace_ref, w1_ref, mf_ref, mw_ref, sums_ref,
    src_ref, rows_ref, vf_ref, vw_ref, lane_ref, tlane_ref, w2_ref, cache_ref, wins_v, wins_s, list_s, upper_ref, lower_ref, spread_ref, sem,
):
    own = tgt_ref.shape[1] // GS
    total = own + 2 * HALO

    reach = HALO * GS
    points = tgt_ref.shape[1]
    for at, field, coords in ((0, bf_ref, bx_ref), (reach, rhs_ref, points_ref), (reach + points, af_ref, ax_ref)):
        src_ref[0:8, at:at + field.shape[1]] = field[...]
        src_ref[8:11, at:at + field.shape[1]] = coords[...]
    src_ref[11:16, :] = jnp.zeros((5, src_ref.shape[1]), f32)

    def clear(g, _):
        rows_ref[:, pl.ds(pl.multiple_of(g * ROW_STRIDE + GS, 8), max(WINS)), :] = jnp.zeros(
            (3, max(WINS), LANES), f32
        )
        vf_ref[:, pl.ds(pl.multiple_of(g * VAL_STRIDE + GS, LANES), 384)] = jnp.zeros((F, 384), f32)
        vw_ref[:, pl.ds(pl.multiple_of(g * VAL_STRIDE, LANES), VAL_STRIDE)] = jnp.zeros((F, VAL_STRIDE), f32)
        return 0

    lax.fori_loop(0, total, clear, 0)
    w2_ref[...] = jnp.zeros_like(w2_ref)
    mf_ref[...] = jnp.zeros_like(mf_ref)
    mw_ref[...] = jnp.zeros_like(mw_ref)

    upper_ref[...] = (iota((SEG, SEG), 0) < iota((SEG, SEG), 1)).astype(f32).astype(bf16)
    lower_ref[...] = (iota((BINS, BINS), 1) < iota((BINS, BINS), 0)).astype(f32).astype(bf16)

    part = iota((16, 3 * LANES), 0)
    spread_ref[...] = ((part < 9) & (part % 3 == iota((16, 3 * LANES), 1) // LANES)).astype(f32).astype(bf16)

    def sort_source(g):
        at = pl.multiple_of(g * GS, GS)
        live = slot_mask(scnt_ref, g)
        values = src_ref[:, pl.ds(at, GS)]
        place, to_lane = order(values[9:10], live, upper_ref, lower_ref)
        splace_ref[:, pl.ds(at, GS)] = place
        pieces = in_order(values[8:11], values[:8], place, to_lane)
        for h, (points, field, _) in enumerate(pieces):
            lane_ref[:, pl.ds(at + h * LANES, LANES)] = points
            vf_ref[:, pl.ds(pl.multiple_of(g * VAL_STRIDE + h * LANES, LANES), LANES)] = field
        parts = jnp.concatenate([piece[2] for piece in pieces], 1).astype(bf16)
        wide = dot(parts, spread_ref[...], ((0,), (0,)))
        for axis in range(3):
            rows_ref[axis, pl.ds(pl.multiple_of(g * ROW_STRIDE, 8), GS), :] = wide[:, axis * LANES:(axis + 1) * LANES]

    def sort_target(g):
        at = pl.multiple_of(g * GS, GS)
        live = slot_mask(tcnt_ref, g)
        points = tgt_ref[:, pl.ds(at, GS)]
        place, to_lane = order(points[1:2], live, upper_ref, lower_ref)
        tplace_ref[:, pl.ds(at, GS)] = place
        for h, (moved, _, _) in enumerate(in_order(points, None, place, to_lane)):
            tlane_ref[:, pl.ds(at + h * LANES, LANES)] = moved

    def several(fn, n):
        def some(i, _):
            for u in range(TOGETHER):
                fn(TOGETHER * i + u)
            return 0

        lax.fori_loop(0, n // TOGETHER, some, 0)

    several(sort_source, total)
    several(sort_target, own)

    def windows(points_ref, at, count, g, acc, column):
        place = iota((8, LANES), 1) + iota((8, LANES), 0) * LANES
        y = jnp.concatenate(
            [points_ref[1:2, pl.ds(at + h * LANES, LANES)] for h in range(CHUNKS)], 0
        )
        low = jnp.min(jnp.where(place < count, y, jnp.inf), axis=1, keepdims=True) - R
        high = jnp.max(jnp.where(place < count, y, -jnp.inf), axis=1, keepdims=True) + R
        packed = jnp.zeros((8, 1), i32)
        steps = jnp.zeros((8, 1), i32)
        for b in range(3):
            there = g + b - 1
            yq = lane_ref[1:2, pl.ds(pl.multiple_of(there * GS, GS), GS)]
            n = live_total(scnt_ref, there)
            slot = jnp.broadcast_to(iota((1, GS), 1), (8, GS))
            near = (yq >= low) & (yq <= high) & (slot < n)
            slot = slot.astype(f32)
            first = jnp.min(jnp.where(near, slot, 4096.0), axis=1, keepdims=True).astype(i32)
            end = jnp.max(jnp.where(near, slot + 1.0, 0.0), axis=1, keepdims=True).astype(i32)
            unit = jnp.where(end > 0, first // 8, 0)
            packed = packed + unit * (128 ** b)
            steps = jnp.maximum(steps, (end - unit * 8 - WINS[b] + MORE - 1) // MORE)
        packed = packed + steps * (128 ** 3)
        return jnp.where(iota((8, LANES), 1) == column, packed, acc)

    def source_windows(g, acc):
        return windows(lane_ref, pl.multiple_of(g * GS, GS), live_total(scnt_ref, g), g, acc, g)

    def target_windows(g, acc):
        return windows(
            tlane_ref, pl.multiple_of(g * GS, GS), live_total(tcnt_ref, g), g + HALO, acc, g + total
        )

    def two(fn, first):
        return lambda i, acc: fn(first + 2 * i + 1, fn(first + 2 * i, acc))

    acc = lax.fori_loop(0, (total - 2) // 2, two(source_windows, 1), jnp.zeros((8, LANES), i32))
    wins_v[...] = lax.fori_loop(0, own // 2, two(target_windows, 0), acc)
    copy = pltpu.make_async_copy(wins_v, wins_s, sem)
    copy.start()
    copy.wait()

    def window_start(packed, b, skip):
        return pl.multiple_of(jnp.minimum(((packed >> (7 * b)) & 127) * 8 + skip, GS), 8)

    def near_phi(points, there, start, width):
        row = pl.multiple_of(there * ROW_STRIDE + start, 8)
        pieces = []
        for r in range(0, width, PIECE):
            square = None
            for axis in range(3):
                offset = rows_ref[axis, pl.ds(row + r, PIECE), :] - points[axis:axis + 1, :]
                square = offset * offset if axis == 0 else square + offset * offset
            square = jnp.minimum(jnp.maximum(square, 1e-30), float(R * R))
            distance = square * lax.rsqrt(square)
            rest = R - distance
            rest = rest * rest
            pieces.append(jnp.concatenate(split(rest * rest * (distance + 1.0)), 1))
        return jnp.concatenate(pieces, 0)

    def near_values(value_refs, there, start, width):
        parts = []
        for ref in value_refs:
            window = ref[:, pl.ds(pl.multiple_of(there * VAL_STRIDE + start // LANES * LANES, LANES), 384)]
            window = pltpu.roll(window, lax.rem(384 - start % LANES, 384), 1)[:, :width]
            parts += list(split(window))
        return jnp.concatenate(parts, 0)

    def interact(points, packed, skips, widths, g, value_refs, keep=None, kept=None):
        acc = None
        for b in range(3):
            width = widths[b]
            start = window_start(packed, b, skips[b])
            rows = slice(WIN_AT[b], WIN_AT[b] + width)
            if kept is None:
                phi = near_phi(points, g + b - 1, start, width)
            else:
                phi = cache_ref[kept, rows, :]
            if keep is not None:
                cache_ref[keep, rows, :] = phi
            term = dot(near_values(value_refs, g + b - 1, start, width), phi)
            acc = term if acc is None else acc + term
        return acc[:, :LANES] + acc[:, LANES:]

    def list_chunks(cnt_ref, first, end):
        def list_group(g, n):
            def list_chunk(c, n):
                list_s[n] = g * CHUNKS + c
                return n + 1

            return lax.fori_loop(0, (live_total(cnt_ref, g) + LANES - 1) // LANES, list_chunk, n)

        return lax.fori_loop(first, end, list_group, 0)

    def work_on(i, n, column0, g0, points_ref, cnt_ref, value_refs, place, keep=False, kept=False):
        work = []
        for u in range(BATCH):
            item = list_s[jnp.minimum(i * BATCH + u, n - 1)]
            g = item // CHUNKS
            c = item % CHUNKS
            at = pl.multiple_of(item * LANES, LANES)
            packed = wins_s[c, g + column0]
            slot = lax.rem(i, LAG + 1) * BATCH + u
            steps = jnp.where(i * BATCH + u < n, packed >> 21, 0)
            work.append((g, c, at, packed, points_ref[:, pl.ds(at, LANES)], slot, steps))
        accs = tuple(
            interact(
                points, packed, (0, 0, 0), WINS, g + g0, value_refs, slot if keep else None, slot if kept else None
            )
            for g, c, at, packed, points, slot, steps in work
        )

        def finish(acc, v, g, c):
            here = (iota((F, LANES), 1) + c * LANES) < live_total(cnt_ref, g)
            out = (acc[16 * v:16 * v + 8] + acc[16 * v + 8:16 * v + 16]) * (1.0 / 256.0)
            return jnp.where(here, out, 0.0)

        for acc, (g, c, at, packed, points, slot, steps) in zip(accs, work):
            for v in range(len(value_refs)):
                place(v, g, c, at)[...] = finish(acc, v, g, c)

        def rest():
            for g, c, at, packed, points, slot, steps in work:

                def more(k, _, g=g, c=c, at=at, packed=packed, points=points):
                    skips = [w + k * MORE for w in WINS]
                    acc = interact(points, packed, skips, (MORE,) * 3, g + g0, value_refs)
                    for v in range(len(value_refs)):
                        place(v, g, c, at)[...] += finish(acc, v, g, c)
                    return 0

                lax.fori_loop(0, steps, more, 0)

        return sum(w[-1] for w in work), rest

    def run_rest(*rests):
        @pl.when(sum(steps for steps, _ in rests) > 0)
        def _():
            for _, rest in rests:
                rest()

    def place_w1(v, g, c, at):
        return vw_ref.at[:, pl.ds(pl.multiple_of(g * VAL_STRIDE + c * LANES, LANES), LANES)]

    def place_w2(v, g, c, at):
        return w2_ref.at[:, pl.ds(at, LANES)]

    n = list_chunks(scnt_ref, 1, total - 1)
    batches = (n + BATCH - 1) // BATCH

    def first_pass(i):
        return work_on(i, n, 0, 0, lane_ref, scnt_ref, [vf_ref], place_w1, keep=True)

    def second_pass(i):
        return work_on(i, n, 0, 0, lane_ref, scnt_ref, [vw_ref], place_w2, kept=True)

    def lead(i, _):
        run_rest(first_pass(i))
        return 0

    def both(i, _):
        run_rest(second_pass(i - LAG), first_pass(i))
        return 0

    def trail(i, _):
        run_rest(second_pass(i - LAG))
        return 0

    lax.fori_loop(0, LAG, lead, 0)
    lax.fori_loop(LAG, batches, both, 0)
    lax.fori_loop(jnp.maximum(batches, LAG), batches + LAG, trail, 0)

    def place_mapped(v, g, c, at):
        return (mf_ref, mw_ref)[v].at[:, pl.ds(at, LANES)]

    n = list_chunks(tcnt_ref, 0, own)

    def mapped_pass(i, _):
        run_rest(work_on(i, n, total, HALO, tlane_ref, tcnt_ref, [vf_ref, vw_ref], place_mapped))
        return 0

    lax.fori_loop(0, (n + BATCH - 1) // BATCH, mapped_pass, 0)

    def first_sums(g, acc):
        ff, fw = acc
        at = pl.multiple_of((g + HALO) * VAL_STRIDE, LANES)
        f = vf_ref[:, pl.ds(at, GS)]
        w = vw_ref[:, pl.ds(at, GS)]
        w1_ref[:, pl.ds(pl.multiple_of(g * GS, GS), GS)] = w
        return ff + f * f, fw + f * w

    zero = jnp.zeros((F, GS), f32)
    ff, fw = lax.fori_loop(0, own, first_sums, (zero, zero))
    ff = jnp.sum(ff, axis=1, keepdims=True)
    fw = jnp.sum(fw, axis=1, keepdims=True)
    shift = jnp.where(ff > 0, fw / jnp.where(ff > 0, ff, 1.0), 0.0)

    def second_sums(g, acc):
        ee, ez, fz = acc
        at = pl.multiple_of((g + HALO) * VAL_STRIDE, LANES)
        f = vf_ref[:, pl.ds(at, GS)]
        w = vw_ref[:, pl.ds(at, GS)]
        e = w - shift * f
        z = w2_ref[:, pl.ds(pl.multiple_of((g + HALO) * GS, GS), GS)] - shift * w
        return ee + e * e, ez + e * z, fz + f * z

    sums = lax.fori_loop(0, own, second_sums, (zero, zero, zero))
    sums = [ff, shift] + [jnp.sum(s, axis=1, keepdims=True) for s in sums]
    tile = jnp.zeros((F, LANES), f32)
    for n, value in enumerate(sums):
        tile = jnp.where(iota((F, LANES), 1) == n, value, tile)
    sums_ref[...] = jnp.concatenate([tile, jnp.zeros((LANES - F, LANES), f32)], 0).T[:8]


def merge(tiles):
    ff, shift, ee, ez, fz = (tiles[:, n, :] for n in range(5))

    def over(x):
        return jnp.sum(x, axis=0, keepdims=True)

    total = over(ff)
    mean = over(ff * shift) / jnp.where(total > 0, total, 1.0)
    delta = shift - mean
    fw = shift * ff
    return [
        total,
        mean,
        over(ee + delta * delta * ff),
        over(ez + delta * (ee + fz) + delta * delta * fw),
        over(fz + delta * fw),
    ]


def finish_kernel(
    scnt_ref, tcnt_ref, sums_ref, rhs_hbm, splace_hbm, tplace_hbm, w1_hbm, mf_hbm, mw_hbm,
    coef_ref, mapped_ref,
    rhs_ref, splace_ref, tplace_ref, w1_ref, mf_ref, mw_ref,
    first, second, local, send1, recv1, send2, recv2,
):
    me = [lax.axis_index(name) for name in AXES]
    sizes = (second.shape[0], first.shape[0])
    own = rhs_ref.shape[1] // GS

    def peer(axis, by):
        return {AXES[axis]: lax.rem(me[axis] + by, sizes[axis])}

    barrier = pltpu.get_barrier_semaphore()
    for axis in (0, 1):
        for by in range(1, sizes[axis]):
            pl.semaphore_signal(
                barrier, inc=1, device_id=peer(axis, by), device_id_type=pl.DeviceIdType.MESH
            )
    loads = [
        pltpu.make_async_copy(here, there, local.at[n])
        for n, (here, there) in enumerate([
            (rhs_hbm, rhs_ref), (splace_hbm, splace_ref), (tplace_hbm, tplace_ref),
            (w1_hbm, w1_ref), (mf_hbm, mf_ref), (mw_hbm, mw_ref),
        ])
    ]
    for load in loads:
        load.start()
    pl.semaphore_wait(barrier, sizes[0] + sizes[1] - 2)

    def exchange(axis, slots, send, recv):
        copies = []
        for by in range(1, sizes[axis]):
            copy = pltpu.make_async_remote_copy(
                src_ref=slots.at[0],
                dst_ref=slots.at[by],
                send_sem=send.at[by],
                recv_sem=recv.at[by],
                device_id=peer(axis, by),
                device_id_type=pl.DeviceIdType.MESH,
            )
            copy.start()
            copies.append(copy)
        return copies

    def restore(g, _):
        at = pl.multiple_of(g * GS, GS)
        w, f, m = (ref[:, pl.ds(at, GS)] for ref in (w1_ref, mf_ref, mw_ref))
        splace = splace_ref[:, pl.ds(pl.multiple_of(at + HALO * GS, GS), GS)]
        tplace = tplace_ref[:, pl.ds(at, GS)]
        slive = slot_mask(scnt_ref, g)
        tlive = slot_mask(tcnt_ref, g)
        for h in range(CHUNKS):
            lanes = slice(h * LANES, (h + 1) * LANES)
            to = pl.ds(at + h * LANES, LANES)
            rhs_ref[:, to] = jnp.where(slive[:, lanes], rhs_ref[:, to], 0.0)
            w1_ref[:, to] = jnp.where(slive[:, lanes], gather(w, splace[:, lanes]), 0.0)
            mf_ref[:, to] = jnp.where(tlive[:, lanes], gather(f, tplace[:, lanes]), 0.0)
            mw_ref[:, to] = jnp.where(tlive[:, lanes], gather(m, tplace[:, lanes]), 0.0)
        return 0

    first[0] = sums_ref[...]
    copies = exchange(1, first, send1, recv1)
    for load in loads:
        load.wait()
    lax.fori_loop(0, own // 4, restore, 0)
    for copy in copies:
        copy.wait()
    part = merge(first[...])
    second[0] = jnp.concatenate(part + [jnp.zeros((3, LANES), f32)], 0)
    copies = exchange(0, second, send2, recv2)
    lax.fori_loop(own // 4, own, restore, 0)
    for copy in copies:
        copy.wait()
    total, mean, e_e, e_ae, _ = merge(second[...])
    alpha0 = 1.0 / mean
    ratio = e_e / total
    beta = alpha0 * alpha0 * ratio
    alpha1 = e_e / (e_ae - alpha0 * ratio * e_e)
    c1 = -alpha1 * alpha0
    c0 = alpha0 + alpha1 * (1.0 + beta)
    scale = jnp.concatenate([c0, c1, jnp.zeros((LANES - 2, LANES), f32)], 0).T[:F]
    c0 = scale[:, 0:1]
    c1 = scale[:, 1:2]

    def combine(g, _):
        at = pl.ds(pl.multiple_of(g * GS, GS), GS)
        coef_ref[:, at] = c0 * rhs_ref[:, at] + c1 * w1_ref[:, at]
        mapped_ref[:, at] = c0 * mf_ref[:, at] + c1 * mw_ref[:, at]
        return 0

    lax.fori_loop(0, own, combine, 0)


def run_local(scnt, tcnt, before, after, rhs, src, tgt):
    points = tgt.shape[1]
    total = points // GS + 2 * HALO
    vmem = pl.BlockSpec(memory_space=pltpu.VMEM)
    smem = pl.BlockSpec(memory_space=pltpu.SMEM)
    return pl.pallas_call(
        local_kernel,
        out_shape=[
            jax.ShapeDtypeStruct((1, total * GS), i32),
            jax.ShapeDtypeStruct((1, points), i32),
            jax.ShapeDtypeStruct((F, points), f32),
            jax.ShapeDtypeStruct((F, points), f32),
            jax.ShapeDtypeStruct((F, points), f32),
            jax.ShapeDtypeStruct((8, LANES), f32),
        ],
        in_specs=[smem, smem] + [vmem] * 7,
        out_specs=[vmem] * 6,
        scratch_shapes=[
            pltpu.VMEM((16, total * GS), f32),
            pltpu.VMEM((3, total * ROW_STRIDE, LANES), f32),
            pltpu.VMEM((F, total * VAL_STRIDE), f32),
            pltpu.VMEM((F, total * VAL_STRIDE), f32),
            pltpu.VMEM((8, total * GS), f32),
            pltpu.VMEM((8, points), f32),
            pltpu.VMEM((F, total * GS), f32),
            pltpu.VMEM(((LAG + 1) * BATCH, sum(WINS), 2 * LANES), bf16),
            pltpu.VMEM((8, LANES), i32),
            pltpu.SMEM((8, LANES), i32),
            pltpu.SMEM((total * CHUNKS,), i32),
            pltpu.VMEM((SEG, SEG), bf16),
            pltpu.VMEM((BINS, BINS), bf16),
            pltpu.VMEM((16, 3 * LANES), bf16),
            pltpu.SemaphoreType.DMA,
        ],
        compiler_params=pltpu.CompilerParams(vmem_limit_bytes=56 * 1024 * 1024),
        name="local",
    )(scnt, tcnt, *before, *after, rhs, src, tgt)


def run_finish(scnt, tcnt, sums, sizes, *arrays):
    vmem = pl.BlockSpec(memory_space=pltpu.VMEM)
    smem = pl.BlockSpec(memory_space=pltpu.SMEM)
    anywhere = pl.BlockSpec(memory_space=pl.ANY)
    semaphores = [pltpu.SemaphoreType.DMA((n,)) for n in (len(arrays), sizes[1], sizes[1], sizes[0], sizes[0])]
    return pl.pallas_call(
        finish_kernel,
        out_shape=[jax.ShapeDtypeStruct(arrays[0].shape, f32)] * 2,
        in_specs=[smem, smem, vmem] + [anywhere] * len(arrays),
        out_specs=[vmem] * 2,
        scratch_shapes=[pltpu.VMEM(a.shape, a.dtype) for a in arrays]
        + [pltpu.VMEM((sizes[1], 8, LANES), f32), pltpu.VMEM((sizes[0], 8, LANES), f32)]
        + semaphores,
        compiler_params=pltpu.CompilerParams(
            vmem_limit_bytes=60 * 1024 * 1024, collective_id=1, has_side_effects=True
        ),
        name="finish",
    )(scnt, tcnt, sums, *arrays)


def halo_kernel(rhs, points, count, bf, bx, bc, af, ax, ac, send, recv):
    reach = HALO * GS
    me = [lax.axis_index(name) for name in AXES]
    sizes = [lax.axis_size(name) for name in AXES]
    peers = sizes[0] * sizes[1]
    here = me[0] * sizes[1] + me[1]

    def at(by):
        place = lax.rem(here + by + peers, peers)
        return (place // sizes[1], lax.rem(place, sizes[1]))

    barrier = pltpu.get_barrier_semaphore()
    for by in (1, -1):
        pl.semaphore_signal(barrier, inc=1, device_id=at(by), device_id_type=pl.DeviceIdType.MESH)
    pl.semaphore_wait(barrier, 2)
    last = pl.ds(rhs.shape[1] - reach, reach)
    first = pl.ds(0, reach)
    copies = []
    for by, moves in (
        (1, ((rhs.at[:, last], bf), (points.at[:, last], bx), (count, bc))),
        (-1, ((rhs.at[:, first], af), (points.at[:, first], ax), (count, ac))),
    ):
        for source, target in moves:
            n = len(copies)
            copy = pltpu.make_async_remote_copy(
                src_ref=source, dst_ref=target, send_sem=send.at[n], recv_sem=recv.at[n],
                device_id=at(by), device_id_type=pl.DeviceIdType.MESH,
            )
            copy.start()
            copies.append(copy)
    for copy in copies:
        copy.wait()


def run_halo(rhs, points, count):
    reach = HALO * GS
    anywhere = pl.BlockSpec(memory_space=pl.ANY)
    side = [
        jax.ShapeDtypeStruct((F, reach), f32),
        jax.ShapeDtypeStruct((3, reach), f32),
        jax.ShapeDtypeStruct(count.shape, i32),
    ]
    return pl.pallas_call(
        halo_kernel,
        out_shape=side * 2,
        in_specs=[anywhere] * 3,
        out_specs=[anywhere] * 6,
        scratch_shapes=[pltpu.SemaphoreType.DMA((6,)), pltpu.SemaphoreType.DMA((6,))],
        compiler_params=pltpu.CompilerParams(collective_id=2, has_side_effects=True),
        name="halo",
    )(rhs, points, count)


def on_device(src_points, tgt_points, src_count, tgt_count, pair_list, pair_total, rhs):
    blocks = HALO * R
    bf, bx, bc, af, ax, ac = run_halo(rhs, src_points, src_count)
    me = lax.axis_index(AXES)
    bc = jnp.where(me > 0, bc[-blocks:], 0)
    ac = jnp.where(me < lax.axis_size(AXES) - 1, ac[:blocks], 0)
    scnt = jnp.concatenate([bc, src_count, ac])
    splace, tplace, w1, mf, mw, sums = run_local(
        scnt, tgt_count, (bf, bx), (af, ax), rhs, src_points, tgt_points
    )
    sizes = [lax.axis_size(name) for name in AXES]
    return run_finish(src_count, tgt_count, sums, sizes, rhs, splace, tplace, w1, mf, mw)


def solution(mesh):
    return jax.shard_map(
        on_device,
        mesh=mesh,
        in_specs=(
            P(None, AXES),
            P(None, AXES),
            P(AXES),
            P(AXES),
            P(None, AXES),
            P(AXES),
            P(None, AXES),
        ),
        out_specs=(P(None, AXES), P(None, AXES)),
        check_vma=False,
    )
```

```python
import jax
import jax.numpy as jnp
from jax import lax
from jax.experimental import pallas as pl
from jax.experimental.pallas import tpu as pltpu
from jax.sharding import PartitionSpec as P

R = 4
BP = 256
F = 8
GS = R * BP
HALO = 2
LANES = 128
CHUNKS = GS // LANES
BINS = 128
WINS = (208, 176, 208)
WIN_AT = (0, 208, 384)
MORE = 64
PIECE = 16
ROW_STRIDE = GS + max(WINS)
VAL_STRIDE = GS + 384
SEG = 256
BATCH = 4
MAPPED_BATCH = 8
LAG = -(-15 // BATCH) + 1
TOGETHER = 4
AXES = ("src", "tgt")
f32 = jnp.float32
bf16 = jnp.bfloat16
i32 = jnp.int32


def iota(shape, dim):
    return lax.broadcasted_iota(i32, shape, dim)


def dot(a, b, dims=((1,), (0,))):
    return lax.dot_general(a, b, (dims, ((), ())), preferred_element_type=f32)


def slot_mask(cnt_ref, group):
    slot = iota((1, GS), 1)
    block = slot // BP
    limit = jnp.zeros((1, GS), i32)
    for k in range(R):
        limit = jnp.where(block == k, cnt_ref[group * R + k], limit)
    return (slot % BP) < limit


def live_total(cnt_ref, group):
    total = cnt_ref[group * R]
    for k in range(1, R):
        total = total + cnt_ref[group * R + k]
    return total


def order(y, live, upper, lower):
    low = jnp.min(jnp.where(live, y, jnp.inf), axis=1, keepdims=True)
    high = jnp.max(jnp.where(live, y, -jnp.inf), axis=1, keepdims=True)
    scale = BINS / jnp.maximum(high - low, 1e-30)
    scaled = jnp.minimum(jnp.maximum((y - low) * scale, 0.0), BINS - 1.0)
    bin_of = jnp.where(live, scaled.astype(i32), BINS)
    members, counts = [], []
    for s in range(GS // SEG):
        member = (bin_of[:, s * SEG:(s + 1) * SEG] == iota((BINS, SEG), 0)).astype(f32)
        members.append(member)
        counts.append(dot(member.astype(bf16), upper[...]))
    totals = [c[:, -1:] + m[:, -1:] for c, m in zip(counts, members)]
    column = iota((BINS, LANES), 1)
    table = jnp.zeros((BINS, LANES), f32)
    for s, t in enumerate(totals):
        table = jnp.where(column == s, t, table)
    base = jnp.sum(dot(lower[...], table.astype(bf16)), axis=1, keepdims=True)
    places = []
    for m, c, t in zip(members, counts, totals):
        places.append(jnp.sum(m * (c + base), axis=0, keepdims=True))
        base = base + t
    place = jnp.concatenate(places, 1).astype(i32)
    within = jnp.where(live, place % LANES, -1)
    to_lane = (within == iota((LANES, GS), 0)).astype(f32).astype(bf16)
    return place, to_lane


def in_order(points, field, place, to_lane):
    first = (points * 0.99609375).astype(bf16).astype(f32)
    second = (points - first).astype(bf16).astype(f32)
    parts = [first, second, points - first - second, jnp.zeros((7, GS), f32)]
    if field is not None:
        high = field.astype(bf16).astype(f32)
        parts += [high, field - high]
    parts = jnp.concatenate(parts, 0).astype(bf16)
    rows = parts.shape[0]
    chunk = jnp.broadcast_to(place // LANES, (16, GS))
    left = []
    for h in range(CHUNKS):
        here = jnp.where(chunk == h, 1.0, 0.0).astype(bf16)
        left += [parts[r:r + 16] * here for r in range(0, rows, 16)]
    moved = dot(jnp.concatenate(left, 0), to_lane, ((1,), (1,)))
    pieces = []
    for h in range(CHUNKS):
        piece = moved[h * rows:(h + 1) * rows]
        points = piece[0:3] + piece[3:6] + piece[6:9]
        points = jnp.concatenate([points, jnp.zeros((5, LANES), f32)], 0)
        pieces.append((points, None if field is None else piece[16:24] + piece[24:32], piece[:16]))
    return pieces


def gather(values, index):
    index = jnp.broadcast_to(index, (8, LANES))
    lane = index % LANES
    tile = index // LANES
    out = jnp.take_along_axis(values[:, :LANES], lane, axis=1)
    for k in range(1, CHUNKS):
        part = jnp.take_along_axis(values[:, k * LANES:(k + 1) * LANES], lane, axis=1)
        out = jnp.where(tile == k, part, out)
    return out


def split(v):
    high = v.astype(bf16)
    return high, (v - high.astype(f32)).astype(bf16)


def local_kernel(
    scnt_ref, tcnt_ref, bf_ref, bx_ref, af_ref, ax_ref, rhs_ref, points_ref, tgt_ref,
    splace_ref, tplace_ref, w1_ref, mf_ref, mw_ref, sums_ref,
    src_ref, rows_ref, vf_ref, vw_ref, lane_ref, tlane_ref, w2_ref, cache_ref, wins_v, wins_s, list_s, upper_ref, lower_ref, spread_ref, sem,
):
    own = tgt_ref.shape[1] // GS
    total = own + 2 * HALO

    reach = HALO * GS
    points = tgt_ref.shape[1]
    for at, field, coords in ((0, bf_ref, bx_ref), (reach, rhs_ref, points_ref), (reach + points, af_ref, ax_ref)):
        src_ref[0:8, at:at + field.shape[1]] = field[...]
        src_ref[8:11, at:at + field.shape[1]] = coords[...]
    src_ref[11:16, :] = jnp.zeros((5, src_ref.shape[1]), f32)

    def clear(g, _):
        rows_ref[:, pl.ds(pl.multiple_of(g * ROW_STRIDE + GS, 8), max(WINS)), :] = jnp.zeros(
            (3, max(WINS), LANES), f32
        )
        vf_ref[:, pl.ds(pl.multiple_of(g * VAL_STRIDE + GS, LANES), 384)] = jnp.zeros((F, 384), f32)
        vw_ref[:, pl.ds(pl.multiple_of(g * VAL_STRIDE, LANES), VAL_STRIDE)] = jnp.zeros((F, VAL_STRIDE), f32)
        return 0

    lax.fori_loop(0, total, clear, 0)
    w2_ref[...] = jnp.zeros_like(w2_ref)
    mf_ref[...] = jnp.zeros_like(mf_ref)
    mw_ref[...] = jnp.zeros_like(mw_ref)

    upper_ref[...] = (iota((SEG, SEG), 0) < iota((SEG, SEG), 1)).astype(f32).astype(bf16)
    lower_ref[...] = (iota((BINS, BINS), 1) < iota((BINS, BINS), 0)).astype(f32).astype(bf16)

    part = iota((16, 3 * LANES), 0)
    spread_ref[...] = ((part < 9) & (part % 3 == iota((16, 3 * LANES), 1) // LANES)).astype(f32).astype(bf16)

    def sort_source(g):
        at = pl.multiple_of(g * GS, GS)
        live = slot_mask(scnt_ref, g)
        values = src_ref[:, pl.ds(at, GS)]
        place, to_lane = order(values[9:10], live, upper_ref, lower_ref)
        splace_ref[:, pl.ds(at, GS)] = place
        pieces = in_order(values[8:11], values[:8], place, to_lane)
        for h, (points, field, _) in enumerate(pieces):
            lane_ref[:, pl.ds(at + h * LANES, LANES)] = points
            vf_ref[:, pl.ds(pl.multiple_of(g * VAL_STRIDE + h * LANES, LANES), LANES)] = field
        parts = jnp.concatenate([piece[2] for piece in pieces], 1).astype(bf16)
        wide = dot(parts, spread_ref[...], ((0,), (0,)))
        for axis in range(3):
            rows_ref[axis, pl.ds(pl.multiple_of(g * ROW_STRIDE, 8), GS), :] = wide[:, axis * LANES:(axis + 1) * LANES]

    def sort_target(g):
        at = pl.multiple_of(g * GS, GS)
        live = slot_mask(tcnt_ref, g)
        points = tgt_ref[:, pl.ds(at, GS)]
        place, to_lane = order(points[1:2], live, upper_ref, lower_ref)
        tplace_ref[:, pl.ds(at, GS)] = place
        for h, (moved, _, _) in enumerate(in_order(points, None, place, to_lane)):
            tlane_ref[:, pl.ds(at + h * LANES, LANES)] = moved

    def several(fn, n):
        def some(i, _):
            for u in range(TOGETHER):
                fn(TOGETHER * i + u)
            return 0

        lax.fori_loop(0, n // TOGETHER, some, 0)

    several(sort_source, total)
    several(sort_target, own)

    def windows(points_ref, at, count, g, acc, column):
        place = iota((8, LANES), 1) + iota((8, LANES), 0) * LANES
        y = jnp.concatenate(
            [points_ref[1:2, pl.ds(at + h * LANES, LANES)] for h in range(CHUNKS)], 0
        )
        low = jnp.min(jnp.where(place < count, y, jnp.inf), axis=1, keepdims=True) - R
        high = jnp.max(jnp.where(place < count, y, -jnp.inf), axis=1, keepdims=True) + R
        packed = jnp.zeros((8, 1), i32)
        steps = jnp.zeros((8, 1), i32)
        for b in range(3):
            there = g + b - 1
            yq = lane_ref[1:2, pl.ds(pl.multiple_of(there * GS, GS), GS)]
            n = live_total(scnt_ref, there)
            slot = jnp.broadcast_to(iota((1, GS), 1), (8, GS))
            near = (yq >= low) & (yq <= high) & (slot < n)
            slot = slot.astype(f32)
            first = jnp.min(jnp.where(near, slot, 4096.0), axis=1, keepdims=True).astype(i32)
            end = jnp.max(jnp.where(near, slot + 1.0, 0.0), axis=1, keepdims=True).astype(i32)
            unit = jnp.where(end > 0, first // 8, 0)
            packed = packed + unit * (128 ** b)
            steps = jnp.maximum(steps, (end - unit * 8 - WINS[b] + MORE - 1) // MORE)
        packed = packed + steps * (128 ** 3)
        return jnp.where(iota((8, LANES), 1) == column, packed, acc)

    def source_windows(g, acc):
        return windows(lane_ref, pl.multiple_of(g * GS, GS), live_total(scnt_ref, g), g, acc, g)

    def target_windows(g, acc):
        return windows(
            tlane_ref, pl.multiple_of(g * GS, GS), live_total(tcnt_ref, g), g + HALO, acc, g + total
        )

    def all_windows(fn, first, count, acc, together):
        def some(i, acc):
            for u in range(together):
                acc = fn(first + together * i + u, acc)
            return acc

        return lax.fori_loop(0, count // together, some, acc)

    acc = all_windows(source_windows, 1, total - 2, jnp.zeros((8, LANES), i32), 6)
    wins_v[...] = all_windows(target_windows, 0, own, acc, 8)
    copy = pltpu.make_async_copy(wins_v, wins_s, sem)
    copy.start()
    copy.wait()

    def window_start(packed, b, skip):
        return pl.multiple_of(jnp.minimum(((packed >> (7 * b)) & 127) * 8 + skip, GS), 8)

    def near_phi(points, there, start, width):
        row = pl.multiple_of(there * ROW_STRIDE + start, 8)
        pieces = []
        for r in range(0, width, PIECE):
            square = None
            for axis in range(3):
                offset = rows_ref[axis, pl.ds(row + r, PIECE), :] - points[axis:axis + 1, :]
                square = offset * offset if axis == 0 else square + offset * offset
            square = jnp.minimum(jnp.maximum(square, 1e-30), float(R * R))
            distance = square * lax.rsqrt(square)
            rest = R - distance
            rest = rest * rest
            pieces.append(jnp.concatenate(split(rest * rest * (distance + 1.0)), 1))
        return jnp.concatenate(pieces, 0)

    def near_values(value_refs, there, start, width):
        parts = []
        for ref in value_refs:
            window = ref[:, pl.ds(pl.multiple_of(there * VAL_STRIDE + start // LANES * LANES, LANES), 384)]
            window = pltpu.roll(window, lax.rem(384 - start % LANES, 384), 1)[:, :width]
            parts += list(split(window))
        return jnp.concatenate(parts, 0)

    def interact(points, packed, skips, widths, g, value_refs, keep=None, kept=None):
        acc = None
        for b in range(3):
            width = widths[b]
            start = window_start(packed, b, skips[b])
            rows = slice(WIN_AT[b], WIN_AT[b] + width)
            if kept is None:
                phi = near_phi(points, g + b - 1, start, width)
            else:
                phi = cache_ref[kept, rows, :]
            if keep is not None:
                cache_ref[keep, rows, :] = phi
            term = dot(near_values(value_refs, g + b - 1, start, width), phi)
            acc = term if acc is None else acc + term
        return acc[:, :LANES] + acc[:, LANES:]

    def list_chunks(cnt_ref, first, end):
        def list_group(g, n):
            def list_chunk(c, n):
                list_s[n] = g * CHUNKS + c
                return n + 1

            return lax.fori_loop(0, (live_total(cnt_ref, g) + LANES - 1) // LANES, list_chunk, n)

        return lax.fori_loop(first, end, list_group, 0)

    def work_on(i, n, column0, g0, points_ref, cnt_ref, value_refs, place, keep=False, kept=False, size=BATCH):
        work = []
        for u in range(size):
            item = list_s[jnp.minimum(i * size + u, n - 1)]
            g = item // CHUNKS
            c = item % CHUNKS
            at = pl.multiple_of(item * LANES, LANES)
            packed = wins_s[c, g + column0]
            slot = lax.rem(i, LAG + 1) * BATCH + u
            steps = jnp.where(i * size + u < n, packed >> 21, 0)
            work.append((g, c, at, packed, points_ref[:, pl.ds(at, LANES)], slot, steps))
        accs = tuple(
            interact(
                points, packed, (0, 0, 0), WINS, g + g0, value_refs, slot if keep else None, slot if kept else None
            )
            for g, c, at, packed, points, slot, steps in work
        )

        def finish(acc, v, g, c):
            here = (iota((F, LANES), 1) + c * LANES) < live_total(cnt_ref, g)
            out = (acc[16 * v:16 * v + 8] + acc[16 * v + 8:16 * v + 16]) * (1.0 / 256.0)
            return jnp.where(here, out, 0.0)

        for acc, (g, c, at, packed, points, slot, steps) in zip(accs, work):
            for v in range(len(value_refs)):
                place(v, g, c, at)[...] = finish(acc, v, g, c)

        def rest():
            for g, c, at, packed, points, slot, steps in work:

                def more(k, _, g=g, c=c, at=at, packed=packed, points=points):
                    skips = [w + k * MORE for w in WINS]
                    acc = interact(points, packed, skips, (MORE,) * 3, g + g0, value_refs)
                    for v in range(len(value_refs)):
                        place(v, g, c, at)[...] += finish(acc, v, g, c)
                    return 0

                lax.fori_loop(0, steps, more, 0)

        return sum(w[-1] for w in work), rest

    def run_rest(*rests):
        @pl.when(sum(steps for steps, _ in rests) > 0)
        def _():
            for _, rest in rests:
                rest()

    def place_w1(v, g, c, at):
        return vw_ref.at[:, pl.ds(pl.multiple_of(g * VAL_STRIDE + c * LANES, LANES), LANES)]

    def place_w2(v, g, c, at):
        return w2_ref.at[:, pl.ds(at, LANES)]

    n = list_chunks(scnt_ref, 1, total - 1)
    batches = (n + BATCH - 1) // BATCH

    def first_pass(i):
        return work_on(i, n, 0, 0, lane_ref, scnt_ref, [vf_ref], place_w1, keep=True)

    def second_pass(i):
        return work_on(i, n, 0, 0, lane_ref, scnt_ref, [vw_ref], place_w2, kept=True)

    def lead(i, _):
        run_rest(first_pass(i))
        return 0

    def both(i, _):
        run_rest(second_pass(i - LAG), first_pass(i))
        return 0

    def trail(i, _):
        run_rest(second_pass(i - LAG))
        return 0

    lax.fori_loop(0, LAG, lead, 0)
    lax.fori_loop(LAG, batches, both, 0)
    lax.fori_loop(jnp.maximum(batches, LAG), batches + LAG, trail, 0)

    def place_mapped(v, g, c, at):
        return (mf_ref, mw_ref)[v].at[:, pl.ds(at, LANES)]

    n = list_chunks(tcnt_ref, 0, own)

    def mapped_pass(i, _):
        run_rest(
            work_on(
                i, n, total, HALO, tlane_ref, tcnt_ref, [vf_ref, vw_ref], place_mapped, size=MAPPED_BATCH
            )
        )
        return 0

    lax.fori_loop(0, (n + MAPPED_BATCH - 1) // MAPPED_BATCH, mapped_pass, 0)

    def first_sums(g, acc):
        ff, fw = acc
        at = pl.multiple_of((g + HALO) * VAL_STRIDE, LANES)
        f = vf_ref[:, pl.ds(at, GS)]
        w = vw_ref[:, pl.ds(at, GS)]
        w1_ref[:, pl.ds(pl.multiple_of(g * GS, GS), GS)] = w
        return ff + f * f, fw + f * w

    zero = jnp.zeros((F, GS), f32)
    ff, fw = lax.fori_loop(0, own, first_sums, (zero, zero))
    ff = jnp.sum(ff, axis=1, keepdims=True)
    fw = jnp.sum(fw, axis=1, keepdims=True)
    shift = jnp.where(ff > 0, fw / jnp.where(ff > 0, ff, 1.0), 0.0)

    def second_sums(g, acc):
        ee, ez, fz = acc
        at = pl.multiple_of((g + HALO) * VAL_STRIDE, LANES)
        f = vf_ref[:, pl.ds(at, GS)]
        w = vw_ref[:, pl.ds(at, GS)]
        e = w - shift * f
        z = w2_ref[:, pl.ds(pl.multiple_of((g + HALO) * GS, GS), GS)] - shift * w
        return ee + e * e, ez + e * z, fz + f * z

    sums = lax.fori_loop(0, own, second_sums, (zero, zero, zero))
    sums = [ff, shift] + [jnp.sum(s, axis=1, keepdims=True) for s in sums]
    tile = jnp.zeros((F, LANES), f32)
    for n, value in enumerate(sums):
        tile = jnp.where(iota((F, LANES), 1) == n, value, tile)
    sums_ref[...] = jnp.concatenate([tile, jnp.zeros((LANES - F, LANES), f32)], 0).T[:8]


def merge(tiles):
    ff, shift, ee, ez, fz = (tiles[:, n, :] for n in range(5))

    def over(x):
        return jnp.sum(x, axis=0, keepdims=True)

    total = over(ff)
    mean = over(ff * shift) / jnp.where(total > 0, total, 1.0)
    delta = shift - mean
    fw = shift * ff
    return [
        total,
        mean,
        over(ee + delta * delta * ff),
        over(ez + delta * (ee + fz) + delta * delta * fw),
        over(fz + delta * fw),
    ]


def finish_kernel(
    scnt_ref, tcnt_ref, sums_ref, rhs_hbm, splace_hbm, tplace_hbm, w1_hbm, mf_hbm, mw_hbm,
    coef_ref, mapped_ref,
    rhs_ref, splace_ref, tplace_ref, w1_ref, mf_ref, mw_ref,
    first, second, local, send1, recv1, send2, recv2,
):
    me = [lax.axis_index(name) for name in AXES]
    sizes = (second.shape[0], first.shape[0])
    own = rhs_ref.shape[1] // GS

    def peer(axis, by):
        return {AXES[axis]: lax.rem(me[axis] + by, sizes[axis])}

    barrier = pltpu.get_barrier_semaphore()
    for axis in (0, 1):
        for by in range(1, sizes[axis]):
            pl.semaphore_signal(
                barrier, inc=1, device_id=peer(axis, by), device_id_type=pl.DeviceIdType.MESH
            )
    loads = [
        pltpu.make_async_copy(here, there, local.at[n])
        for n, (here, there) in enumerate([
            (rhs_hbm, rhs_ref), (splace_hbm, splace_ref), (tplace_hbm, tplace_ref),
            (w1_hbm, w1_ref), (mf_hbm, mf_ref), (mw_hbm, mw_ref),
        ])
    ]
    for load in loads:
        load.start()
    pl.semaphore_wait(barrier, sizes[0] + sizes[1] - 2)

    def exchange(axis, slots, send, recv):
        copies = []
        for by in range(1, sizes[axis]):
            copy = pltpu.make_async_remote_copy(
                src_ref=slots.at[0],
                dst_ref=slots.at[by],
                send_sem=send.at[by],
                recv_sem=recv.at[by],
                device_id=peer(axis, by),
                device_id_type=pl.DeviceIdType.MESH,
            )
            copy.start()
            copies.append(copy)
        return copies

    def restore(g, _):
        at = pl.multiple_of(g * GS, GS)
        w, f, m = (ref[:, pl.ds(at, GS)] for ref in (w1_ref, mf_ref, mw_ref))
        splace = splace_ref[:, pl.ds(pl.multiple_of(at + HALO * GS, GS), GS)]
        tplace = tplace_ref[:, pl.ds(at, GS)]
        slive = slot_mask(scnt_ref, g)
        tlive = slot_mask(tcnt_ref, g)
        for h in range(CHUNKS):
            lanes = slice(h * LANES, (h + 1) * LANES)
            to = pl.ds(at + h * LANES, LANES)
            rhs_ref[:, to] = jnp.where(slive[:, lanes], rhs_ref[:, to], 0.0)
            w1_ref[:, to] = jnp.where(slive[:, lanes], gather(w, splace[:, lanes]), 0.0)
            mf_ref[:, to] = jnp.where(tlive[:, lanes], gather(f, tplace[:, lanes]), 0.0)
            mw_ref[:, to] = jnp.where(tlive[:, lanes], gather(m, tplace[:, lanes]), 0.0)
        return 0

    first[0] = sums_ref[...]
    copies = exchange(1, first, send1, recv1)
    for load in loads:
        load.wait()
    lax.fori_loop(0, own // 4, restore, 0)
    for copy in copies:
        copy.wait()
    part = merge(first[...])
    second[0] = jnp.concatenate(part + [jnp.zeros((3, LANES), f32)], 0)
    copies = exchange(0, second, send2, recv2)
    lax.fori_loop(own // 4, own, restore, 0)
    for copy in copies:
        copy.wait()
    total, mean, e_e, e_ae, _ = merge(second[...])
    alpha0 = 1.0 / mean
    ratio = e_e / total
    beta = alpha0 * alpha0 * ratio
    alpha1 = e_e / (e_ae - alpha0 * ratio * e_e)
    c1 = -alpha1 * alpha0
    c0 = alpha0 + alpha1 * (1.0 + beta)
    scale = jnp.concatenate([c0, c1, jnp.zeros((LANES - 2, LANES), f32)], 0).T[:F]
    c0 = scale[:, 0:1]
    c1 = scale[:, 1:2]

    def combine(g, _):
        at = pl.ds(pl.multiple_of(g * GS, GS), GS)
        coef_ref[:, at] = c0 * rhs_ref[:, at] + c1 * w1_ref[:, at]
        mapped_ref[:, at] = c0 * mf_ref[:, at] + c1 * mw_ref[:, at]
        return 0

    lax.fori_loop(0, own, combine, 0)


def run_local(scnt, tcnt, before, after, rhs, src, tgt):
    points = tgt.shape[1]
    total = points // GS + 2 * HALO
    vmem = pl.BlockSpec(memory_space=pltpu.VMEM)
    smem = pl.BlockSpec(memory_space=pltpu.SMEM)
    return pl.pallas_call(
        local_kernel,
        out_shape=[
            jax.ShapeDtypeStruct((1, total * GS), i32),
            jax.ShapeDtypeStruct((1, points), i32),
            jax.ShapeDtypeStruct((F, points), f32),
            jax.ShapeDtypeStruct((F, points), f32),
            jax.ShapeDtypeStruct((F, points), f32),
            jax.ShapeDtypeStruct((8, LANES), f32),
        ],
        in_specs=[smem, smem] + [vmem] * 7,
        out_specs=[vmem] * 6,
        scratch_shapes=[
            pltpu.VMEM((16, total * GS), f32),
            pltpu.VMEM((3, total * ROW_STRIDE, LANES), f32),
            pltpu.VMEM((F, total * VAL_STRIDE), f32),
            pltpu.VMEM((F, total * VAL_STRIDE), f32),
            pltpu.VMEM((8, total * GS), f32),
            pltpu.VMEM((8, points), f32),
            pltpu.VMEM((F, total * GS), f32),
            pltpu.VMEM(((LAG + 1) * BATCH, sum(WINS), 2 * LANES), bf16),
            pltpu.VMEM((8, LANES), i32),
            pltpu.SMEM((8, LANES), i32),
            pltpu.SMEM((total * CHUNKS,), i32),
            pltpu.VMEM((SEG, SEG), bf16),
            pltpu.VMEM((BINS, BINS), bf16),
            pltpu.VMEM((16, 3 * LANES), bf16),
            pltpu.SemaphoreType.DMA,
        ],
        compiler_params=pltpu.CompilerParams(vmem_limit_bytes=56 * 1024 * 1024),
        name="local",
    )(scnt, tcnt, *before, *after, rhs, src, tgt)


def run_finish(scnt, tcnt, sums, sizes, *arrays):
    vmem = pl.BlockSpec(memory_space=pltpu.VMEM)
    smem = pl.BlockSpec(memory_space=pltpu.SMEM)
    anywhere = pl.BlockSpec(memory_space=pl.ANY)
    semaphores = [pltpu.SemaphoreType.DMA((n,)) for n in (len(arrays), sizes[1], sizes[1], sizes[0], sizes[0])]
    return pl.pallas_call(
        finish_kernel,
        out_shape=[jax.ShapeDtypeStruct(arrays[0].shape, f32)] * 2,
        in_specs=[smem, smem, vmem] + [anywhere] * len(arrays),
        out_specs=[vmem] * 2,
        scratch_shapes=[pltpu.VMEM(a.shape, a.dtype) for a in arrays]
        + [pltpu.VMEM((sizes[1], 8, LANES), f32), pltpu.VMEM((sizes[0], 8, LANES), f32)]
        + semaphores,
        compiler_params=pltpu.CompilerParams(
            vmem_limit_bytes=60 * 1024 * 1024, collective_id=1, has_side_effects=True
        ),
        name="finish",
    )(scnt, tcnt, sums, *arrays)


def halo_kernel(rhs, points, count, bf, bx, bc, af, ax, ac, send, recv):
    reach = HALO * GS
    me = [lax.axis_index(name) for name in AXES]
    sizes = [lax.axis_size(name) for name in AXES]
    peers = sizes[0] * sizes[1]
    here = me[0] * sizes[1] + me[1]

    def at(by):
        place = lax.rem(here + by + peers, peers)
        return (place // sizes[1], lax.rem(place, sizes[1]))

    barrier = pltpu.get_barrier_semaphore()
    for by in (1, -1):
        pl.semaphore_signal(barrier, inc=1, device_id=at(by), device_id_type=pl.DeviceIdType.MESH)
    pl.semaphore_wait(barrier, 2)
    last = pl.ds(rhs.shape[1] - reach, reach)
    first = pl.ds(0, reach)
    copies = []
    for by, moves in (
        (1, ((rhs.at[:, last], bf), (points.at[:, last], bx), (count, bc))),
        (-1, ((rhs.at[:, first], af), (points.at[:, first], ax), (count, ac))),
    ):
        for source, target in moves:
            n = len(copies)
            copy = pltpu.make_async_remote_copy(
                src_ref=source, dst_ref=target, send_sem=send.at[n], recv_sem=recv.at[n],
                device_id=at(by), device_id_type=pl.DeviceIdType.MESH,
            )
            copy.start()
            copies.append(copy)
    for copy in copies:
        copy.wait()


def run_halo(rhs, points, count):
    reach = HALO * GS
    anywhere = pl.BlockSpec(memory_space=pl.ANY)
    side = [
        jax.ShapeDtypeStruct((F, reach), f32),
        jax.ShapeDtypeStruct((3, reach), f32),
        jax.ShapeDtypeStruct(count.shape, i32),
    ]
    return pl.pallas_call(
        halo_kernel,
        out_shape=side * 2,
        in_specs=[anywhere] * 3,
        out_specs=[anywhere] * 6,
        scratch_shapes=[pltpu.SemaphoreType.DMA((6,)), pltpu.SemaphoreType.DMA((6,))],
        compiler_params=pltpu.CompilerParams(collective_id=2, has_side_effects=True),
        name="halo",
    )(rhs, points, count)


def on_device(src_points, tgt_points, src_count, tgt_count, pair_list, pair_total, rhs):
    blocks = HALO * R
    bf, bx, bc, af, ax, ac = run_halo(rhs, src_points, src_count)
    me = lax.axis_index(AXES)
    bc = jnp.where(me > 0, bc[-blocks:], 0)
    ac = jnp.where(me < lax.axis_size(AXES) - 1, ac[:blocks], 0)
    scnt = jnp.concatenate([bc, src_count, ac])
    splace, tplace, w1, mf, mw, sums = run_local(
        scnt, tgt_count, (bf, bx), (af, ax), rhs, src_points, tgt_points
    )
    sizes = [lax.axis_size(name) for name in AXES]
    return run_finish(src_count, tgt_count, sums, sizes, rhs, splace, tplace, w1, mf, mw)


def solution(mesh):
    return jax.shard_map(
        on_device,
        mesh=mesh,
        in_specs=(
            P(None, AXES),
            P(None, AXES),
            P(AXES),
            P(AXES),
            P(None, AXES),
            P(AXES),
            P(None, AXES),
        ),
        out_specs=(P(None, AXES), P(None, AXES)),
        check_vma=False,
    )
```

```python
import jax
import jax.numpy as jnp
from jax import lax
from jax.experimental import pallas as pl
from jax.experimental.pallas import tpu as pltpu
from jax.sharding import PartitionSpec as P

R = 4
BP = 256
F = 8
GS = R * BP
HALO = 2
LANES = 128
CHUNKS = GS // LANES
BINS = 128
WINS = (208, 176, 208)
WIN_AT = (0, 208, 384)
MORE = 64
PIECE = 16
ROW_STRIDE = GS + max(WINS)
VAL_STRIDE = GS + 384
SEG = 256
BATCH = 4
MAPPED_BATCH = 8
LAG = -(-15 // BATCH) + 1
TOGETHER = 4
AXES = ("src", "tgt")
f32 = jnp.float32
bf16 = jnp.bfloat16
i32 = jnp.int32


def iota(shape, dim):
    return lax.broadcasted_iota(i32, shape, dim)


def dot(a, b, dims=((1,), (0,))):
    return lax.dot_general(a, b, (dims, ((), ())), preferred_element_type=f32)


def slot_mask(cnt_ref, group):
    slot = iota((1, GS), 1)
    block = slot // BP
    limit = jnp.zeros((1, GS), i32)
    for k in range(R):
        limit = jnp.where(block == k, cnt_ref[group * R + k], limit)
    return (slot % BP) < limit


def live_total(cnt_ref, group):
    total = cnt_ref[group * R]
    for k in range(1, R):
        total = total + cnt_ref[group * R + k]
    return total


def order(y, live, upper, lower):
    low = jnp.min(jnp.where(live, y, jnp.inf), axis=1, keepdims=True)
    high = jnp.max(jnp.where(live, y, -jnp.inf), axis=1, keepdims=True)
    scale = BINS / jnp.maximum(high - low, 1e-30)
    scaled = jnp.minimum(jnp.maximum((y - low) * scale, 0.0), BINS - 1.0)
    bin_of = jnp.where(live, scaled.astype(i32), BINS)
    members, counts = [], []
    for s in range(GS // SEG):
        member = (bin_of[:, s * SEG:(s + 1) * SEG] == iota((BINS, SEG), 0)).astype(f32)
        members.append(member)
        counts.append(dot(member.astype(bf16), upper[...]))
    totals = [c[:, -1:] + m[:, -1:] for c, m in zip(counts, members)]
    column = iota((BINS, LANES), 1)
    table = jnp.zeros((BINS, LANES), f32)
    for s, t in enumerate(totals):
        table = jnp.where(column == s, t, table)
    base = jnp.sum(dot(lower[...], table.astype(bf16)), axis=1, keepdims=True)
    places = []
    for m, c, t in zip(members, counts, totals):
        places.append(jnp.sum(m * (c + base), axis=0, keepdims=True))
        base = base + t
    place = jnp.concatenate(places, 1).astype(i32)
    within = jnp.where(live, place % LANES, -1)
    to_lane = (within == iota((LANES, GS), 0)).astype(f32).astype(bf16)
    return place, to_lane


def in_order(points, field, place, to_lane):
    first = (points * 0.99609375).astype(bf16).astype(f32)
    second = (points - first).astype(bf16).astype(f32)
    parts = [first, second, points - first - second, jnp.zeros((7, GS), f32)]
    if field is not None:
        high = field.astype(bf16).astype(f32)
        parts += [high, field - high]
    parts = jnp.concatenate(parts, 0).astype(bf16)
    rows = parts.shape[0]
    chunk = jnp.broadcast_to(place // LANES, (16, GS))
    left = []
    for h in range(CHUNKS):
        here = jnp.where(chunk == h, 1.0, 0.0).astype(bf16)
        left += [parts[r:r + 16] * here for r in range(0, rows, 16)]
    moved = dot(jnp.concatenate(left, 0), to_lane, ((1,), (1,)))
    pieces = []
    for h in range(CHUNKS):
        piece = moved[h * rows:(h + 1) * rows]
        points = piece[0:3] + piece[3:6] + piece[6:9]
        points = jnp.concatenate([points, jnp.zeros((5, LANES), f32)], 0)
        pieces.append((points, None if field is None else piece[16:24] + piece[24:32], piece[:16]))
    return pieces


def gather(values, index):
    index = jnp.broadcast_to(index, (8, LANES))
    lane = index % LANES
    tile = index // LANES
    out = jnp.take_along_axis(values[:, :LANES], lane, axis=1)
    for k in range(1, CHUNKS):
        part = jnp.take_along_axis(values[:, k * LANES:(k + 1) * LANES], lane, axis=1)
        out = jnp.where(tile == k, part, out)
    return out


def split(v):
    high = v.astype(bf16)
    return high, (v - high.astype(f32)).astype(bf16)


def local_kernel(
    me_ref, bc_ref, cnt_ref, ac_ref, tcnt_ref, bf_ref, bx_ref, af_ref, ax_ref, rhs_ref, points_ref, tgt_ref,
    splace_ref, tplace_ref, w1_ref, mf_ref, mw_ref, sums_ref,
    src_ref, rows_ref, vf_ref, vw_ref, lane_ref, tlane_ref, w2_ref, cache_ref, wins_v, wins_s, list_s, upper_ref, lower_ref, spread_ref, scnt_ref, sem,
):
    blocks = HALO * R
    inner = cnt_ref.shape[0]

    def own_count(i, _):
        scnt_ref[blocks + i] = cnt_ref[i]
        return 0

    lax.fori_loop(0, inner, own_count, 0)
    for i in range(blocks):
        scnt_ref[i] = jnp.where(me_ref[0] > 0, bc_ref[inner - blocks + i], 0)
        scnt_ref[blocks + inner + i] = jnp.where(me_ref[0] < lax.axis_size(AXES) - 1, ac_ref[i], 0)
    own = tgt_ref.shape[1] // GS
    total = own + 2 * HALO

    reach = HALO * GS
    points = tgt_ref.shape[1]
    for at, field, coords in ((0, bf_ref, bx_ref), (reach, rhs_ref, points_ref), (reach + points, af_ref, ax_ref)):
        src_ref[0:8, at:at + field.shape[1]] = field[...]
        src_ref[8:11, at:at + field.shape[1]] = coords[...]
    src_ref[11:16, :] = jnp.zeros((5, src_ref.shape[1]), f32)

    def clear(g, _):
        rows_ref[:, pl.ds(pl.multiple_of(g * ROW_STRIDE + GS, 8), max(WINS)), :] = jnp.zeros(
            (3, max(WINS), LANES), f32
        )
        vf_ref[:, pl.ds(pl.multiple_of(g * VAL_STRIDE + GS, LANES), 384)] = jnp.zeros((F, 384), f32)
        vw_ref[:, pl.ds(pl.multiple_of(g * VAL_STRIDE, LANES), VAL_STRIDE)] = jnp.zeros((F, VAL_STRIDE), f32)
        return 0

    lax.fori_loop(0, total, clear, 0)
    w2_ref[...] = jnp.zeros_like(w2_ref)
    mf_ref[...] = jnp.zeros_like(mf_ref)
    mw_ref[...] = jnp.zeros_like(mw_ref)

    upper_ref[...] = (iota((SEG, SEG), 0) < iota((SEG, SEG), 1)).astype(f32).astype(bf16)
    lower_ref[...] = (iota((BINS, BINS), 1) < iota((BINS, BINS), 0)).astype(f32).astype(bf16)

    part = iota((16, 3 * LANES), 0)
    spread_ref[...] = ((part < 9) & (part % 3 == iota((16, 3 * LANES), 1) // LANES)).astype(f32).astype(bf16)

    def sort_source(g):
        at = pl.multiple_of(g * GS, GS)
        live = slot_mask(scnt_ref, g)
        values = src_ref[:, pl.ds(at, GS)]
        place, to_lane = order(values[9:10], live, upper_ref, lower_ref)
        splace_ref[:, pl.ds(at, GS)] = place
        pieces = in_order(values[8:11], values[:8], place, to_lane)
        for h, (points, field, _) in enumerate(pieces):
            lane_ref[:, pl.ds(at + h * LANES, LANES)] = points
            vf_ref[:, pl.ds(pl.multiple_of(g * VAL_STRIDE + h * LANES, LANES), LANES)] = field
        parts = jnp.concatenate([piece[2] for piece in pieces], 1).astype(bf16)
        wide = dot(parts, spread_ref[...], ((0,), (0,)))
        for axis in range(3):
            rows_ref[axis, pl.ds(pl.multiple_of(g * ROW_STRIDE, 8), GS), :] = wide[:, axis * LANES:(axis + 1) * LANES]

    def sort_target(g):
        at = pl.multiple_of(g * GS, GS)
        live = slot_mask(tcnt_ref, g)
        points = tgt_ref[:, pl.ds(at, GS)]
        place, to_lane = order(points[1:2], live, upper_ref, lower_ref)
        tplace_ref[:, pl.ds(at, GS)] = place
        for h, (moved, _, _) in enumerate(in_order(points, None, place, to_lane)):
            tlane_ref[:, pl.ds(at + h * LANES, LANES)] = moved

    def several(fn, n):
        def some(i, _):
            for u in range(TOGETHER):
                fn(TOGETHER * i + u)
            return 0

        lax.fori_loop(0, n // TOGETHER, some, 0)

    several(sort_source, total)
    several(sort_target, own)

    def windows(points_ref, at, count, g, acc, column):
        place = iota((8, LANES), 1) + iota((8, LANES), 0) * LANES
        y = jnp.concatenate(
            [points_ref[1:2, pl.ds(at + h * LANES, LANES)] for h in range(CHUNKS)], 0
        )
        low = jnp.min(jnp.where(place < count, y, jnp.inf), axis=1, keepdims=True) - R
        high = jnp.max(jnp.where(place < count, y, -jnp.inf), axis=1, keepdims=True) + R
        packed = jnp.zeros((8, 1), i32)
        steps = jnp.zeros((8, 1), i32)
        for b in range(3):
            there = g + b - 1
            yq = lane_ref[1:2, pl.ds(pl.multiple_of(there * GS, GS), GS)]
            n = live_total(scnt_ref, there)
            slot = jnp.broadcast_to(iota((1, GS), 1), (8, GS))
            near = (yq >= low) & (yq <= high) & (slot < n)
            slot = slot.astype(f32)
            first = jnp.min(jnp.where(near, slot, 4096.0), axis=1, keepdims=True).astype(i32)
            end = jnp.max(jnp.where(near, slot + 1.0, 0.0), axis=1, keepdims=True).astype(i32)
            unit = jnp.where(end > 0, first // 8, 0)
            packed = packed + unit * (128 ** b)
            steps = jnp.maximum(steps, (end - unit * 8 - WINS[b] + MORE - 1) // MORE)
        packed = packed + steps * (128 ** 3)
        return jnp.where(iota((8, LANES), 1) == column, packed, acc)

    def source_windows(g, acc):
        return windows(lane_ref, pl.multiple_of(g * GS, GS), live_total(scnt_ref, g), g, acc, g)

    def target_windows(g, acc):
        return windows(
            tlane_ref, pl.multiple_of(g * GS, GS), live_total(tcnt_ref, g), g + HALO, acc, g + total
        )

    def all_windows(fn, first, count, acc, together):
        def some(i, acc):
            for u in range(together):
                acc = fn(first + together * i + u, acc)
            return acc

        return lax.fori_loop(0, count // together, some, acc)

    acc = all_windows(source_windows, 1, total - 2, jnp.zeros((8, LANES), i32), 6)
    wins_v[...] = all_windows(target_windows, 0, own, acc, 8)
    copy = pltpu.make_async_copy(wins_v, wins_s, sem)
    copy.start()
    copy.wait()

    def window_start(packed, b, skip):
        return pl.multiple_of(jnp.minimum(((packed >> (7 * b)) & 127) * 8 + skip, GS), 8)

    def near_phi(points, there, start, width):
        row = pl.multiple_of(there * ROW_STRIDE + start, 8)
        pieces = []
        for r in range(0, width, PIECE):
            square = None
            for axis in range(3):
                offset = rows_ref[axis, pl.ds(row + r, PIECE), :] - points[axis:axis + 1, :]
                square = offset * offset if axis == 0 else square + offset * offset
            square = jnp.minimum(jnp.maximum(square, 1e-30), float(R * R))
            distance = square * lax.rsqrt(square)
            rest = R - distance
            rest = rest * rest
            pieces.append(jnp.concatenate(split(rest * rest * (distance + 1.0)), 1))
        return jnp.concatenate(pieces, 0)

    def near_values(value_refs, there, start, width):
        parts = []
        for ref in value_refs:
            window = ref[:, pl.ds(pl.multiple_of(there * VAL_STRIDE + start // LANES * LANES, LANES), 384)]
            window = pltpu.roll(window, lax.rem(384 - start % LANES, 384), 1)[:, :width]
            parts += list(split(window))
        return jnp.concatenate(parts, 0)

    def interact(points, packed, skips, widths, g, value_refs, keep=None, kept=None):
        acc = None
        for b in range(3):
            width = widths[b]
            start = window_start(packed, b, skips[b])
            rows = slice(WIN_AT[b], WIN_AT[b] + width)
            if kept is None:
                phi = near_phi(points, g + b - 1, start, width)
            else:
                phi = cache_ref[kept, rows, :]
            if keep is not None:
                cache_ref[keep, rows, :] = phi
            term = dot(near_values(value_refs, g + b - 1, start, width), phi)
            acc = term if acc is None else acc + term
        return acc[:, :LANES] + acc[:, LANES:]

    def list_chunks(cnt_ref, first, end):
        def list_group(g, n):
            def list_chunk(c, n):
                list_s[n] = g * CHUNKS + c
                return n + 1

            return lax.fori_loop(0, (live_total(cnt_ref, g) + LANES - 1) // LANES, list_chunk, n)

        return lax.fori_loop(first, end, list_group, 0)

    def work_on(i, n, column0, g0, points_ref, cnt_ref, value_refs, place, keep=False, kept=False, size=BATCH):
        work = []
        for u in range(size):
            item = list_s[jnp.minimum(i * size + u, n - 1)]
            g = item // CHUNKS
            c = item % CHUNKS
            at = pl.multiple_of(item * LANES, LANES)
            packed = wins_s[c, g + column0]
            slot = lax.rem(i, LAG + 1) * BATCH + u
            steps = jnp.where(i * size + u < n, packed >> 21, 0)
            work.append((g, c, at, packed, points_ref[:, pl.ds(at, LANES)], slot, steps))
        accs = tuple(
            interact(
                points, packed, (0, 0, 0), WINS, g + g0, value_refs, slot if keep else None, slot if kept else None
            )
            for g, c, at, packed, points, slot, steps in work
        )

        def finish(acc, v, g, c):
            here = (iota((F, LANES), 1) + c * LANES) < live_total(cnt_ref, g)
            out = (acc[16 * v:16 * v + 8] + acc[16 * v + 8:16 * v + 16]) * (1.0 / 256.0)
            return jnp.where(here, out, 0.0)

        for acc, (g, c, at, packed, points, slot, steps) in zip(accs, work):
            for v in range(len(value_refs)):
                place(v, g, c, at)[...] = finish(acc, v, g, c)

        def rest():
            for g, c, at, packed, points, slot, steps in work:

                def more(k, _, g=g, c=c, at=at, packed=packed, points=points):
                    skips = [w + k * MORE for w in WINS]
                    acc = interact(points, packed, skips, (MORE,) * 3, g + g0, value_refs)
                    for v in range(len(value_refs)):
                        place(v, g, c, at)[...] += finish(acc, v, g, c)
                    return 0

                lax.fori_loop(0, steps, more, 0)

        return sum(w[-1] for w in work), rest

    def run_rest(*rests):
        @pl.when(sum(steps for steps, _ in rests) > 0)
        def _():
            for _, rest in rests:
                rest()

    def place_w1(v, g, c, at):
        return vw_ref.at[:, pl.ds(pl.multiple_of(g * VAL_STRIDE + c * LANES, LANES), LANES)]

    def place_w2(v, g, c, at):
        return w2_ref.at[:, pl.ds(at, LANES)]

    n = list_chunks(scnt_ref, 1, total - 1)
    batches = (n + BATCH - 1) // BATCH

    def first_pass(i):
        return work_on(i, n, 0, 0, lane_ref, scnt_ref, [vf_ref], place_w1, keep=True)

    def second_pass(i):
        return work_on(i, n, 0, 0, lane_ref, scnt_ref, [vw_ref], place_w2, kept=True)

    def lead(i, _):
        run_rest(first_pass(i))
        return 0

    def both(i, _):
        run_rest(second_pass(i - LAG), first_pass(i))
        return 0

    def trail(i, _):
        run_rest(second_pass(i - LAG))
        return 0

    lax.fori_loop(0, LAG, lead, 0)
    lax.fori_loop(LAG, batches, both, 0)
    lax.fori_loop(jnp.maximum(batches, LAG), batches + LAG, trail, 0)

    def place_mapped(v, g, c, at):
        return (mf_ref, mw_ref)[v].at[:, pl.ds(at, LANES)]

    n = list_chunks(tcnt_ref, 0, own)

    def mapped_pass(i, _):
        run_rest(
            work_on(
                i, n, total, HALO, tlane_ref, tcnt_ref, [vf_ref, vw_ref], place_mapped, size=MAPPED_BATCH
            )
        )
        return 0

    lax.fori_loop(0, (n + MAPPED_BATCH - 1) // MAPPED_BATCH, mapped_pass, 0)

    def first_sums(g, acc):
        ff, fw = acc
        at = pl.multiple_of((g + HALO) * VAL_STRIDE, LANES)
        f = vf_ref[:, pl.ds(at, GS)]
        w = vw_ref[:, pl.ds(at, GS)]
        w1_ref[:, pl.ds(pl.multiple_of(g * GS, GS), GS)] = w
        return ff + f * f, fw + f * w

    zero = jnp.zeros((F, GS), f32)
    ff, fw = lax.fori_loop(0, own, first_sums, (zero, zero))
    ff = jnp.sum(ff, axis=1, keepdims=True)
    fw = jnp.sum(fw, axis=1, keepdims=True)
    shift = jnp.where(ff > 0, fw / jnp.where(ff > 0, ff, 1.0), 0.0)

    def second_sums(g, acc):
        ee, ez, fz = acc
        at = pl.multiple_of((g + HALO) * VAL_STRIDE, LANES)
        f = vf_ref[:, pl.ds(at, GS)]
        w = vw_ref[:, pl.ds(at, GS)]
        e = w - shift * f
        z = w2_ref[:, pl.ds(pl.multiple_of((g + HALO) * GS, GS), GS)] - shift * w
        return ee + e * e, ez + e * z, fz + f * z

    sums = lax.fori_loop(0, own, second_sums, (zero, zero, zero))
    sums = [ff, shift] + [jnp.sum(s, axis=1, keepdims=True) for s in sums]
    tile = jnp.zeros((F, LANES), f32)
    for n, value in enumerate(sums):
        tile = jnp.where(iota((F, LANES), 1) == n, value, tile)
    sums_ref[...] = jnp.concatenate([tile, jnp.zeros((LANES - F, LANES), f32)], 0).T[:8]


def merge(tiles):
    ff, shift, ee, ez, fz = (tiles[:, n, :] for n in range(5))

    def over(x):
        return jnp.sum(x, axis=0, keepdims=True)

    total = over(ff)
    mean = over(ff * shift) / jnp.where(total > 0, total, 1.0)
    delta = shift - mean
    fw = shift * ff
    return [
        total,
        mean,
        over(ee + delta * delta * ff),
        over(ez + delta * (ee + fz) + delta * delta * fw),
        over(fz + delta * fw),
    ]


def finish_kernel(
    scnt_ref, tcnt_ref, sums_ref, rhs_hbm, splace_hbm, tplace_hbm, w1_hbm, mf_hbm, mw_hbm,
    coef_ref, mapped_ref,
    rhs_ref, splace_ref, tplace_ref, w1_ref, mf_ref, mw_ref,
    first, second, local, send1, recv1, send2, recv2,
):
    me = [lax.axis_index(name) for name in AXES]
    sizes = (second.shape[0], first.shape[0])
    own = rhs_ref.shape[1] // GS

    def peer(axis, by):
        return {AXES[axis]: lax.rem(me[axis] + by, sizes[axis])}

    barrier = pltpu.get_barrier_semaphore()
    for axis in (0, 1):
        for by in range(1, sizes[axis]):
            pl.semaphore_signal(
                barrier, inc=1, device_id=peer(axis, by), device_id_type=pl.DeviceIdType.MESH
            )
    loads = [
        pltpu.make_async_copy(here, there, local.at[n])
        for n, (here, there) in enumerate([
            (rhs_hbm, rhs_ref), (splace_hbm, splace_ref), (tplace_hbm, tplace_ref),
            (w1_hbm, w1_ref), (mf_hbm, mf_ref), (mw_hbm, mw_ref),
        ])
    ]
    for load in loads:
        load.start()
    pl.semaphore_wait(barrier, sizes[0] + sizes[1] - 2)

    def exchange(axis, slots, send, recv):
        copies = []
        for by in range(1, sizes[axis]):
            copy = pltpu.make_async_remote_copy(
                src_ref=slots.at[0],
                dst_ref=slots.at[by],
                send_sem=send.at[by],
                recv_sem=recv.at[by],
                device_id=peer(axis, by),
                device_id_type=pl.DeviceIdType.MESH,
            )
            copy.start()
            copies.append(copy)
        return copies

    def restore(g, _):
        at = pl.multiple_of(g * GS, GS)
        w, f, m = (ref[:, pl.ds(at, GS)] for ref in (w1_ref, mf_ref, mw_ref))
        splace = splace_ref[:, pl.ds(pl.multiple_of(at + HALO * GS, GS), GS)]
        tplace = tplace_ref[:, pl.ds(at, GS)]
        slive = slot_mask(scnt_ref, g)
        tlive = slot_mask(tcnt_ref, g)
        for h in range(CHUNKS):
            lanes = slice(h * LANES, (h + 1) * LANES)
            to = pl.ds(at + h * LANES, LANES)
            rhs_ref[:, to] = jnp.where(slive[:, lanes], rhs_ref[:, to], 0.0)
            w1_ref[:, to] = jnp.where(slive[:, lanes], gather(w, splace[:, lanes]), 0.0)
            mf_ref[:, to] = jnp.where(tlive[:, lanes], gather(f, tplace[:, lanes]), 0.0)
            mw_ref[:, to] = jnp.where(tlive[:, lanes], gather(m, tplace[:, lanes]), 0.0)
        return 0

    first[0] = sums_ref[...]
    copies = exchange(1, first, send1, recv1)
    for load in loads:
        load.wait()
    lax.fori_loop(0, own // 4, restore, 0)
    for copy in copies:
        copy.wait()
    part = merge(first[...])
    second[0] = jnp.concatenate(part + [jnp.zeros((3, LANES), f32)], 0)
    copies = exchange(0, second, send2, recv2)
    lax.fori_loop(own // 4, own, restore, 0)
    for copy in copies:
        copy.wait()
    total, mean, e_e, e_ae, _ = merge(second[...])
    alpha0 = 1.0 / mean
    ratio = e_e / total
    beta = alpha0 * alpha0 * ratio
    alpha1 = e_e / (e_ae - alpha0 * ratio * e_e)
    c1 = -alpha1 * alpha0
    c0 = alpha0 + alpha1 * (1.0 + beta)
    scale = jnp.concatenate([c0, c1, jnp.zeros((LANES - 2, LANES), f32)], 0).T[:F]
    c0 = scale[:, 0:1]
    c1 = scale[:, 1:2]

    def combine(g, _):
        at = pl.ds(pl.multiple_of(g * GS, GS), GS)
        coef_ref[:, at] = c0 * rhs_ref[:, at] + c1 * w1_ref[:, at]
        mapped_ref[:, at] = c0 * mf_ref[:, at] + c1 * mw_ref[:, at]
        return 0

    lax.fori_loop(0, own, combine, 0)


def run_local(me, bc, cnt, ac, tcnt, before, after, rhs, src, tgt):
    points = tgt.shape[1]
    total = points // GS + 2 * HALO
    vmem = pl.BlockSpec(memory_space=pltpu.VMEM)
    smem = pl.BlockSpec(memory_space=pltpu.SMEM)
    return pl.pallas_call(
        local_kernel,
        out_shape=[
            jax.ShapeDtypeStruct((1, total * GS), i32),
            jax.ShapeDtypeStruct((1, points), i32),
            jax.ShapeDtypeStruct((F, points), f32),
            jax.ShapeDtypeStruct((F, points), f32),
            jax.ShapeDtypeStruct((F, points), f32),
            jax.ShapeDtypeStruct((8, LANES), f32),
        ],
        in_specs=[smem] * 5 + [vmem] * 7,
        out_specs=[vmem] * 6,
        scratch_shapes=[
            pltpu.VMEM((16, total * GS), f32),
            pltpu.VMEM((3, total * ROW_STRIDE, LANES), f32),
            pltpu.VMEM((F, total * VAL_STRIDE), f32),
            pltpu.VMEM((F, total * VAL_STRIDE), f32),
            pltpu.VMEM((8, total * GS), f32),
            pltpu.VMEM((8, points), f32),
            pltpu.VMEM((F, total * GS), f32),
            pltpu.VMEM(((LAG + 1) * BATCH, sum(WINS), 2 * LANES), bf16),
            pltpu.VMEM((8, LANES), i32),
            pltpu.SMEM((8, LANES), i32),
            pltpu.SMEM((total * CHUNKS,), i32),
            pltpu.VMEM((SEG, SEG), bf16),
            pltpu.VMEM((BINS, BINS), bf16),
            pltpu.VMEM((16, 3 * LANES), bf16),
            pltpu.SMEM((total * R,), i32),
            pltpu.SemaphoreType.DMA,
        ],
        compiler_params=pltpu.CompilerParams(vmem_limit_bytes=56 * 1024 * 1024),
        name="local",
    )(me, bc, cnt, ac, tcnt, *before, *after, rhs, src, tgt)


def run_finish(scnt, tcnt, sums, sizes, *arrays):
    vmem = pl.BlockSpec(memory_space=pltpu.VMEM)
    smem = pl.BlockSpec(memory_space=pltpu.SMEM)
    anywhere = pl.BlockSpec(memory_space=pl.ANY)
    semaphores = [pltpu.SemaphoreType.DMA((n,)) for n in (len(arrays), sizes[1], sizes[1], sizes[0], sizes[0])]
    return pl.pallas_call(
        finish_kernel,
        out_shape=[jax.ShapeDtypeStruct(arrays[0].shape, f32)] * 2,
        in_specs=[smem, smem, vmem] + [anywhere] * len(arrays),
        out_specs=[vmem] * 2,
        scratch_shapes=[pltpu.VMEM(a.shape, a.dtype) for a in arrays]
        + [pltpu.VMEM((sizes[1], 8, LANES), f32), pltpu.VMEM((sizes[0], 8, LANES), f32)]
        + semaphores,
        compiler_params=pltpu.CompilerParams(
            vmem_limit_bytes=60 * 1024 * 1024, collective_id=1, has_side_effects=True
        ),
        name="finish",
    )(scnt, tcnt, sums, *arrays)


def halo_kernel(rhs, points, count, bf, bx, bc, af, ax, ac, send, recv):
    reach = HALO * GS
    me = [lax.axis_index(name) for name in AXES]
    sizes = [lax.axis_size(name) for name in AXES]
    peers = sizes[0] * sizes[1]
    here = me[0] * sizes[1] + me[1]

    def at(by):
        place = lax.rem(here + by + peers, peers)
        return (place // sizes[1], lax.rem(place, sizes[1]))

    barrier = pltpu.get_barrier_semaphore()
    for by in (1, -1):
        pl.semaphore_signal(barrier, inc=1, device_id=at(by), device_id_type=pl.DeviceIdType.MESH)
    pl.semaphore_wait(barrier, 2)
    last = pl.ds(rhs.shape[1] - reach, reach)
    first = pl.ds(0, reach)
    copies = []
    for by, moves in (
        (1, ((rhs.at[:, last], bf), (points.at[:, last], bx), (count, bc))),
        (-1, ((rhs.at[:, first], af), (points.at[:, first], ax), (count, ac))),
    ):
        for source, target in moves:
            n = len(copies)
            copy = pltpu.make_async_remote_copy(
                src_ref=source, dst_ref=target, send_sem=send.at[n], recv_sem=recv.at[n],
                device_id=at(by), device_id_type=pl.DeviceIdType.MESH,
            )
            copy.start()
            copies.append(copy)
    for copy in copies:
        copy.wait()


def run_halo(rhs, points, count):
    reach = HALO * GS
    anywhere = pl.BlockSpec(memory_space=pl.ANY)
    side = [
        jax.ShapeDtypeStruct((F, reach), f32),
        jax.ShapeDtypeStruct((3, reach), f32),
        jax.ShapeDtypeStruct(count.shape, i32),
    ]
    return pl.pallas_call(
        halo_kernel,
        out_shape=side * 2,
        in_specs=[anywhere] * 3,
        out_specs=[anywhere] * 6,
        scratch_shapes=[pltpu.SemaphoreType.DMA((6,)), pltpu.SemaphoreType.DMA((6,))],
        compiler_params=pltpu.CompilerParams(collective_id=2, has_side_effects=True),
        name="halo",
    )(rhs, points, count)


def on_device(src_points, tgt_points, src_count, tgt_count, pair_list, pair_total, rhs):
    bf, bx, bc, af, ax, ac = run_halo(rhs, src_points, src_count)
    me = lax.axis_index(AXES).astype(i32)[None]
    splace, tplace, w1, mf, mw, sums = run_local(
        me, bc, src_count, ac, tgt_count, (bf, bx), (af, ax), rhs, src_points, tgt_points
    )
    sizes = [lax.axis_size(name) for name in AXES]
    return run_finish(src_count, tgt_count, sums, sizes, rhs, splace, tplace, w1, mf, mw)


def solution(mesh):
    return jax.shard_map(
        on_device,
        mesh=mesh,
        in_specs=(
            P(None, AXES),
            P(None, AXES),
            P(AXES),
            P(AXES),
            P(None, AXES),
            P(AXES),
            P(None, AXES),
        ),
        out_specs=(P(None, AXES), P(None, AXES)),
        check_vma=False,
    )
```
